32 devices in a mesh: groups: 2 (over y), width: 4 (over z), tokens: 4 (over x, core).
Axes of the slice: x: 2, y: 2, z: 4, core: 2. Of those that a mesh axis runs over, the one named last changes fastest.
Arguments:
- layer_inputs: bfloat16 [4096, 27648], P(('groups', 'tokens'), 'width'), parts along dimension 0, may hold values from -6 to 6
- output_grads: bfloat16 [4096, 5120], P(('groups', 'tokens'), 'width'), parts along dimension 0, may hold values from -6 to 6
- proj_in: bfloat16 [32, 27648], P(None, 'width'), may hold values from -0.0390625 to 0.0390625
- proj_out: bfloat16 [32, 5120], P(None, 'width'), may hold values from -0.078125 to 0.078125
- prior_gram: float32 [2048, 1024], P(('groups', 'tokens'), 'width'), parts along dimension 0, may hold values from 0 to 512, as said below
- query_bank: float32 [256, 1024], P(('groups', 'tokens')), parts along dimension 0, may hold values from -6 to 6
- slab_sequence: int32 [32], P('groups'), parts along dimension 0, may hold values from 0 to 15, each once
- seq_lengths: int32 [32], P('groups'), parts along dimension 0, may hold values from 16 to 128
- query_ids: int32 [256], P('groups'), parts along dimension 0, may hold values from 0 to 127, as said below
Outputs:
- scores: float32 [256, 16], P(('groups', 'tokens'), 'width'), parts along dimension 0
The draws below stay inside these ranges and needn't reach their ends.
There are 2 independent parts, one for each index of `groups`. The reference program is written for one: setup_inputs(seed, part) draws one part's arguments, and reference() takes and returns one part's arrays. A program takes and returns all parts, laid end to end along the dimension named above; an argument that names none is the same for every part. Nothing has to cross between parts.
Inputs may be any that keep to these rules, and one draw needn't show every extreme that they name: `prior_gram`: symmetric and positive semidefinite. `slab_sequence`: each sequence number names exactly one slab. `query_ids`: ids may repeat.
All inputs are finite; a program needn't handle non-finite values.
Results may differ from the reference program's by a relative error of at most 0.0003.
Values sent between devices are 32-bit elements; how exact they have to be, the bound alone decides.
No kernel may reach another device: no remote copies, remote signals or barrier semaphores. Data moves between devices by JAX's collectives and lax.ppermute only.
A program may use at most 128 MiB of HBM per device.

```python
import math
import jax
import jax.numpy as jnp
from jax import lax

DIN = 27648
DOUT = 5120
R_IN = 32
R_OUT = 32
SEQ_LEN = 128
K = 1024
TOKENS = 2048
NSEQ = 16
NQ = 128
QBANK = 128


def draw_prior_gram(key, part):
    key = jax.random.fold_in(key, 17)
    first_key, second_key = jax.random.split(key)
    spots = jax.random.uniform(first_key, (K,), jnp.float32, 0.0, 40.0)
    row_scale = jnp.exp(jax.random.uniform(second_key, (K,), jnp.float32, 0.0, math.log(2.0)))
    kernel = jnp.exp(-jnp.abs(spots[:, None] - spots[None, :]))
    return 0.5 * SEQ_LEN * kernel * row_scale[:, None] * row_scale[None, :]


def draw_seq_lengths(key, part):
    key = jax.random.fold_in(key, 29)
    first_key, second_key, third_key = jax.random.split(key, 3)
    drawn_values = jax.random.randint(first_key, (NSEQ,), SEQ_LEN // 8, SEQ_LEN + 1, dtype=jnp.int32)
    long_slot = jax.random.randint(second_key, (), 0, NSEQ, dtype=jnp.int32)
    short_slot = (long_slot + 1 + jax.random.randint(third_key, (), 0, NSEQ - 1, dtype=jnp.int32)) % NSEQ
    return drawn_values.at[long_slot].set(SEQ_LEN).at[short_slot].set(SEQ_LEN // 8)


def draw_query_ids(key, part):
    key = jax.random.fold_in(key, 41)
    first_key, second_key, third_key = jax.random.split(key, 3)
    drawn_values = jax.random.randint(first_key, (NQ,), 0, QBANK, dtype=jnp.int32)
    high_slot = jax.random.randint(second_key, (), 0, NQ, dtype=jnp.int32)
    low_slot = (high_slot + 1 + jax.random.randint(third_key, (), 0, NQ - 1, dtype=jnp.int32)) % NQ
    return drawn_values.at[high_slot].set(QBANK - 1).at[low_slot].set(0)


def steps_of(key, shape, pieces, low, largest):
    def one(dim, parts):
        heights = jax.random.uniform(jax.random.fold_in(jax.random.fold_in(key, 6), dim), (parts,), jnp.float32, low / len(pieces), largest / len(pieces))
        return jnp.repeat(jnp.exp(heights), shape[dim] // parts).reshape((-1,) + (1,) * (len(shape) - dim - 1))

    factor_of = one(*pieces[0])
    for cut in pieces[1:]:
        factor_of = factor_of * one(*cut)
    return factor_of


def noise(own_key, dims, scale, limit, cuts=(), held_as=jnp.bfloat16):
    array = scale * jax.random.normal(own_key, dims, jnp.float32)
    if cuts:
        array = array * steps_of(own_key, dims, cuts, -0.22, 0.18)
    return jnp.clip(array, -limit, limit).astype(held_as)


def setup_inputs(seed: int = 0, part: int = 0) -> dict:
    splits = jax.random.split(jax.random.key(seed), 10)
    part_splits = jax.random.split(jax.random.fold_in(splits[9], part), 10)
    return {
        "layer_inputs": noise(part_splits[0], (TOKENS, DIN), 1.0, 6.0, ((0, 4), (1, 4))),
        "output_grads": noise(part_splits[1], (TOKENS, DOUT), 1.0, 6.0, ((0, 4), (1, 4))),
        "proj_in": noise(splits[2], (R_IN, DIN), DIN ** -0.5, 0.0390625, ((1, 4),)),
        "proj_out": noise(splits[3], (R_OUT, DOUT), DOUT ** -0.5, 0.078125, ((1, 4),)),
        "prior_gram": draw_prior_gram(jax.random.fold_in(jax.random.fold_in(splits[9], part), 71), part),
        "query_bank": noise(part_splits[5], (QBANK, K), (4 * (SEQ_LEN / K) ** 0.5), 6.0, ((0, 4),), jnp.float32),
        "slab_sequence": jax.random.permutation(part_splits[6], NSEQ).astype(jnp.int32),
        "seq_lengths": draw_seq_lengths(jax.random.fold_in(jax.random.fold_in(splits[9], part), 71), part),
        "query_ids": draw_query_ids(jax.random.fold_in(jax.random.fold_in(splits[9], part), 71), part),
    }


def reference(layer_inputs, output_grads, proj_in, proj_out, prior_gram, query_bank, slab_sequence, seq_lengths, query_ids):
    contract = (((1,), (1,)), ((), ()))
    in_proj = lax.dot_general(layer_inputs.astype(jnp.float32), proj_in.astype(jnp.float32), contract, preferred_element_type=jnp.float32)
    out_proj = lax.dot_general(output_grads.astype(jnp.float32), proj_out.astype(jnp.float32), contract, preferred_element_type=jnp.float32)
    in_slabs = in_proj.reshape(NSEQ, SEQ_LEN, R_IN)
    out_slabs = out_proj.reshape(NSEQ, SEQ_LEN, R_OUT)
    slab_lengths = seq_lengths[slab_sequence]
    valid_mask = (jnp.arange(SEQ_LEN)[None, :] < slab_lengths[:, None]).astype(jnp.float32)
    slab_grads = jnp.einsum('nla,nlb->nab', in_slabs * valid_mask[:, :, None], out_slabs, precision=lax.Precision.HIGHEST).reshape(NSEQ, K)
    seq_grads = jnp.zeros((NSEQ, K), jnp.float32).at[slab_sequence].set(slab_grads)
    gram_total = prior_gram + jnp.dot(seq_grads.T, seq_grads, precision=lax.Precision.HIGHEST) / NSEQ
    damped = gram_total + 0.1 * jnp.trace(gram_total) / K * jnp.eye(K, dtype=jnp.float32)
    factor = jnp.linalg.cholesky(damped)
    solved = jax.scipy.linalg.cho_solve((factor, True), seq_grads.T)
    queries = query_bank[query_ids]
    return jnp.dot(queries, solved, precision=lax.Precision.HIGHEST)
```

```python
import jax
import jax.numpy as jnp
from jax import lax
from jax.experimental import pallas as pl
from jax.experimental.pallas import tpu as pltpu
from jax.sharding import PartitionSpec as P

R_IN = 32
SEQ_LEN = 128
K = 1024
BLOCK = 128
PIVOTS = 16
TERMS = 6
f32 = jnp.float32


damping_ratio = 0.1
highest = lax.Precision.HIGHEST


def split_terms(value):
    high = value.astype(jnp.bfloat16)
    rest = value - high.astype(f32)
    mid = rest.astype(jnp.bfloat16)
    low = (rest - mid.astype(f32)).astype(jnp.bfloat16)
    return high, mid, low


def left_terms(value, axis):
    high, mid, low = split_terms(value)
    return jnp.concatenate([high, high, mid, mid, high, low], axis)


def right_terms(value, axis):
    high, mid, low = split_terms(value)
    return jnp.concatenate([high, mid, high, mid, low, high], axis)


def both_terms(value, axis):
    high, mid, low = split_terms(value)
    return (
        jnp.concatenate([high, high, mid, mid, high, low], axis),
        jnp.concatenate([high, mid, high, mid, low, high], axis),
    )


def contract(a, b, a_dim, b_dim):
    return lax.dot_general(a, b, (((a_dim,), (b_dim,)), ((), ())), preferred_element_type=f32)


def eye_mask():
    shape = (BLOCK, BLOCK)
    return lax.broadcasted_iota(jnp.int32, shape, 0) == lax.broadcasted_iota(jnp.int32, shape, 1)


def factor_block(work):
    work[:, BLOCK:] = eye_mask().astype(f32)
    tiles = PIVOTS // 8
    row = lax.broadcasted_iota(jnp.int32, (8, 2 * BLOCK), 0)
    for group in range(BLOCK // PIVOTS):
        base = group * PIVOTS
        rows = [work[base + 8 * h : base + 8 * h + 8, :] for h in range(tiles)]
        columns = [
            [
                jnp.broadcast_to(
                    work[base + 8 * h : base + 8 * h + 8, base + j : base + j + 1], (8, BLOCK)
                )
                for h in range(tiles)
            ]
            for j in range(PIVOTS)
        ]
        for j in range(PIVOTS):
            hj, jj = divmod(j, 8)
            scale = lax.rsqrt(jnp.broadcast_to(columns[j][hj][jj : jj + 1, :], (8, BLOCK)))
            lower = [columns[j][h] * scale for h in range(hj, tiles)]
            pivot_row = jnp.broadcast_to(rows[hj][jj : jj + 1, :], (8, 2 * BLOCK)) * jnp.concatenate(
                [scale, scale], 1
            )
            for l in range(j + 1, PIVOTS):
                entry = jnp.broadcast_to(columns[l][hj][jj : jj + 1, :], (8, BLOCK)) * scale
                for h in range(hj, tiles):
                    columns[l][h] = columns[l][h] - lower[h - hj] * entry
            for h in range(hj, tiles):
                wide = jnp.concatenate([lower[h - hj], lower[h - hj]], 1)
                changed = rows[h] - wide * pivot_row
                if h == hj:
                    changed = jnp.where(
                        row > jj, changed, jnp.where(row == jj, pivot_row, rows[h])
                    )
                rows[h] = changed
        done = jnp.concatenate(rows, 0)
        work[base : base + PIVOTS, :] = done
        if base + PIVOTS < BLOCK:
            left, right = both_terms(done, 0)
            change = contract(left[:, :BLOCK], right, 0, 0)
            work[base + PIVOTS :, :] = work[base + PIVOTS :, :] - change[base + PIVOTS :, :]


def solve_kernel(prior_ref, grads_ref, query_ref, out_ref, gram, extra, work, left_ref, right_ref):
    size = gram.shape[0]
    blocks = size // BLOCK
    part_rows, part_cols = prior_ref.shape[2:]
    sequences = grads_ref.shape[0]
    grads = grads_ref[...]
    on_diagonal = eye_mask()

    def prior_block(i, j):
        r, c = i * BLOCK, j * BLOCK
        return prior_ref[
            r // part_rows,
            c // part_cols,
            r % part_rows : r % part_rows + BLOCK,
            c % part_cols : c % part_cols + BLOCK,
        ]

    diagonal = jnp.zeros((BLOCK, BLOCK), f32)
    for i in range(blocks):
        diagonal = diagonal + jnp.where(on_diagonal, prior_block(i, i), 0.0)
    trace = jnp.sum(diagonal) + jnp.sum(grads * grads) / sequences
    damping = damping_ratio * trace / size
    left, right = both_terms(grads, 0)
    for i in range(blocks):
        low = i * BLOCK
        product = contract(left[:, low : low + BLOCK], right[:, low:], 0, 0) / sequences
        for j in range(i, blocks):
            value = prior_block(i, j) + product[:, (j - i) * BLOCK : (j - i + 1) * BLOCK]
            if i == j:
                value = value + jnp.where(on_diagonal, damping, 0.0)
            gram[low : low + BLOCK, j * BLOCK : (j + 1) * BLOCK] = value
    extra[:sequences, :] = grads
    extra[sequences:, :] = query_ref[...]
    scores = jnp.zeros(out_ref.shape, f32)
    for k in range(blocks):
        low, high = k * BLOCK, (k + 1) * BLOCK
        work[:, :BLOCK] = gram[low:high, low:high]
        factor_block(work)
        inverse_left, inverse_right = both_terms(work[:, BLOCK:], 1)
        solved = contract(left_terms(extra[:, low:high], 1), inverse_right, 1, 1)
        solved_left, solved_right = both_terms(solved, 1)
        scores = scores + contract(solved_left[sequences:], solved_right[:sequences], 1, 1)
        if k == blocks - 1:
            break
        panel = contract(inverse_left, right_terms(gram[low:high, high:], 0), 1, 0)
        panel_left, panel_right = both_terms(panel, 0)
        left_ref[:, high:] = panel_left
        right_ref[:, high:] = panel_right
        extra[:, high:] = extra[:, high:] - contract(solved_left, panel_right, 1, 0)
        for i in range(high, size, BLOCK):
            gram[i : i + BLOCK, i:] = gram[i : i + BLOCK, i:] - contract(
                left_ref[:, i : i + BLOCK], right_ref[:, i:], 0, 0
            )
    out_ref[...] = scores


def solve(prior_parts, grads, queries):
    size = grads.shape[1]
    rows = grads.shape[0] + queries.shape[0]
    return pl.pallas_call(
        solve_kernel,
        out_shape=jax.ShapeDtypeStruct((queries.shape[0], grads.shape[0]), f32),
        scratch_shapes=[
            pltpu.VMEM((size, size), f32),
            pltpu.VMEM((rows, size), f32),
            pltpu.VMEM((BLOCK, 2 * BLOCK), f32),
            pltpu.VMEM((TERMS * BLOCK, size), jnp.bfloat16),
            pltpu.VMEM((TERMS * BLOCK, size), jnp.bfloat16),
        ],
        compiler_params=pltpu.CompilerParams(vmem_limit_bytes=48 * 2**20),
        cost_estimate=pl.CostEstimate(
            flops=4 * size**3, bytes_accessed=4 * size * size, transcendentals=size
        ),
    )(prior_parts, grads, queries)


def slab_sums(projected, first_row, local_lengths, slab_count):
    row_count = projected.shape[1]
    position = first_row + jnp.arange(row_count, dtype=jnp.int32)
    slab_index = position // SEQ_LEN
    offset = position - slab_index * SEQ_LEN
    owners = jnp.arange(slab_count, dtype=jnp.int32)
    weights = jnp.where(
        (slab_index[None, :] == owners[:, None]) & (offset[None, :] < local_lengths[:, None]),
        1.0,
        0.0,
    ).astype(jnp.float32)
    masked = weights[:, None, :] * projected[None, :R_IN, :]
    products = lax.dot_general(
        masked, projected[R_IN:, :], (((2,), (1,)), ((), ())), precision=highest
    )
    return products.reshape(slab_count, K)


def local(
    layer_inputs,
    output_grads,
    proj_in,
    proj_out,
    prior_gram,
    query_bank,
    slab_sequence,
    seq_lengths,
    query_ids,
):
    width_count = lax.axis_size("width")
    token_count = lax.axis_size("tokens")
    tok_rows = layer_inputs.shape[0]
    slab_count = tok_rows // SEQ_LEN
    sequence_count = slab_sequence.shape[0]
    features = (((1,), (1,)), ((), ()))
    projected = jnp.concatenate(
        [
            lax.dot_general(proj_in, layer_inputs, features, preferred_element_type=jnp.float32),
            lax.dot_general(proj_out, output_grads, features, preferred_element_type=jnp.float32),
        ],
        axis=0,
    )
    local_slabs = lax.dynamic_slice_in_dim(
        slab_sequence, lax.axis_index("tokens") * slab_count, slab_count
    )
    seq_numbers = jnp.arange(sequence_count, dtype=jnp.int32)
    local_lengths = jnp.sum(
        jnp.where(local_slabs[:, None] == seq_numbers[None, :], seq_lengths[None, :], 0), axis=1
    )
    shared = lax.psum_scatter(projected, "width", scatter_dimension=1, tiled=True)
    partial_value = slab_sums(
        shared, lax.axis_index("width") * shared.shape[1], local_lengths, slab_count
    )
    vectors = lax.psum(partial_value, "width")
    prior_block = lax.all_gather(prior_gram, "width", axis=0)
    prior_parts = lax.all_gather(prior_block, "tokens", axis=0)
    if prior_gram.shape[1] % BLOCK or prior_gram.shape[0] % BLOCK:
        prior_parts = prior_parts.transpose(0, 2, 1, 3).reshape(1, 1, K, K)
    all_grads = lax.all_gather(vectors, "tokens", axis=0, tiled=True)
    bank_block = solve(prior_parts, all_grads, query_bank)
    column_count = sequence_count // width_count
    column_ids = lax.axis_index("width") * column_count + jnp.arange(column_count, dtype=jnp.int32)
    chooser = (slab_sequence[:, None] == column_ids[None, :]).astype(jnp.float32)
    bank_block = jnp.dot(bank_block, chooser, precision=highest)
    query_count = query_ids.shape[0] // token_count
    local_ids = lax.dynamic_slice_in_dim(
        query_ids, lax.axis_index("tokens") * query_count, query_count
    )
    all_scores = lax.all_gather(bank_block, "tokens", axis=0, tiled=True)
    bank_index = jnp.arange(all_scores.shape[0], dtype=jnp.int32)
    onehot = (local_ids[:, None] == bank_index[None, :]).astype(jnp.float32)
    return jnp.dot(onehot, all_scores, precision=highest)


def solution(mesh):
    return jax.shard_map(
        local,
        mesh=mesh,
        in_specs=(
            P(("groups", "tokens"), "width"),
            P(("groups", "tokens"), "width"),
            P(None, "width"),
            P(None, "width"),
            P(("groups", "tokens"), "width"),
            P(("groups", "tokens"), None),
            P("groups"),
            P("groups"),
            P("groups"),
        ),
        out_specs=P(("groups", "tokens"), "width"),
        check_vma=False,
    )
```

```python
import functools

import jax
import jax.numpy as jnp
from jax import lax
from jax.experimental import pallas as pl
from jax.experimental.pallas import tpu as pltpu
from jax.sharding import PartitionSpec as P

R_IN = 32
SEQ_LEN = 128
K = 1024
BLOCK = 128
PIVOTS = 16
TERMS = 6
f32 = jnp.float32


damping_ratio = 0.1
highest = lax.Precision.HIGHEST


def split_terms(value):
    high = value.astype(jnp.bfloat16)
    rest = value - high.astype(f32)
    mid = rest.astype(jnp.bfloat16)
    low = (rest - mid.astype(f32)).astype(jnp.bfloat16)
    return high, mid, low


def left_terms(value, axis):
    high, mid, low = split_terms(value)
    return jnp.concatenate([high, high, mid, mid, high, low], axis)


def right_terms(value, axis):
    high, mid, low = split_terms(value)
    return jnp.concatenate([high, mid, high, mid, low, high], axis)


def both_terms(value, axis):
    high, mid, low = split_terms(value)
    return (
        jnp.concatenate([high, high, mid, mid, high, low], axis),
        jnp.concatenate([high, mid, high, mid, low, high], axis),
    )


def contract(a, b, a_dim, b_dim):
    return lax.dot_general(a, b, (((a_dim,), (b_dim,)), ((), ())), preferred_element_type=f32)


def eye_mask():
    shape = (BLOCK, BLOCK)
    return lax.broadcasted_iota(jnp.int32, shape, 0) == lax.broadcasted_iota(jnp.int32, shape, 1)


def factor_block(work):
    work[:, BLOCK:] = eye_mask().astype(f32)
    tiles = PIVOTS // 8
    row = lax.broadcasted_iota(jnp.int32, (8, 2 * BLOCK), 0)
    for group in range(BLOCK // PIVOTS):
        base = group * PIVOTS
        rows = [work[base + 8 * h : base + 8 * h + 8, :] for h in range(tiles)]
        columns = [
            [
                jnp.broadcast_to(
                    work[base + 8 * h : base + 8 * h + 8, base + j : base + j + 1], (8, BLOCK)
                )
                for h in range(tiles)
            ]
            for j in range(PIVOTS)
        ]
        for j in range(PIVOTS):
            hj, jj = divmod(j, 8)
            scale = lax.rsqrt(jnp.broadcast_to(columns[j][hj][jj : jj + 1, :], (8, BLOCK)))
            lower = [columns[j][h] * scale for h in range(hj, tiles)]
            pivot_row = jnp.broadcast_to(rows[hj][jj : jj + 1, :], (8, 2 * BLOCK)) * jnp.concatenate(
                [scale, scale], 1
            )
            for l in range(j + 1, PIVOTS):
                entry = jnp.broadcast_to(columns[l][hj][jj : jj + 1, :], (8, BLOCK)) * scale
                for h in range(hj, tiles):
                    columns[l][h] = columns[l][h] - lower[h - hj] * entry
            for h in range(hj, tiles):
                wide = jnp.concatenate([lower[h - hj], lower[h - hj]], 1)
                changed = rows[h] - wide * pivot_row
                if h == hj:
                    changed = jnp.where(
                        row > jj, changed, jnp.where(row == jj, pivot_row, rows[h])
                    )
                rows[h] = changed
        done = jnp.concatenate(rows, 0)
        work[base : base + PIVOTS, :] = done
        if base + PIVOTS < BLOCK:
            left, right = both_terms(done, 0)
            change = contract(left[:, :BLOCK], right, 0, 0)
            work[base + PIVOTS :, :] = work[base + PIVOTS :, :] - change[base + PIVOTS :, :]


def half_payload(prior, row_part, col_part):
    first, second = prior[:BLOCK, :BLOCK], prior[BLOCK:, BLOCK:]
    upper = eye_mask() | (
        lax.broadcasted_iota(jnp.int32, (BLOCK, BLOCK), 0)
        < lax.broadcasted_iota(jnp.int32, (BLOCK, BLOCK), 1)
    )
    packed = jnp.concatenate([jnp.where(upper, first, second), prior[:BLOCK, BLOCK:]], 1)
    half = jnp.where(
        row_part == col_part,
        packed,
        jnp.where(row_part < col_part, prior[:BLOCK, :], prior[:, BLOCK:].T),
    )
    diagonal = jnp.sum(jnp.where(eye_mask(), second, 0.0), axis=0)
    return jnp.concatenate([half, jnp.zeros((8, 2 * BLOCK), f32).at[0, :BLOCK].set(diagonal)], 0)


def exchange(value, axis):
    count = lax.axis_size(axis)
    return [value] + [
        lax.ppermute(value, axis, [(i, i ^ s) for i in range(count)]) for s in range(1, count)
    ]


def solve_kernel(halves, ids_ref, *refs):
    if halves:
        parts_ref, grads_ref, choose_ref, out_ref = refs[:4]
        gram, extra, work, left_ref, right_ref, tails, bank, sems = refs[4:]
    else:
        prior_ref, bank_ref, grads_ref, choose_ref, out_ref = refs[:5]
        gram, extra, work, left_ref, right_ref, bank, sems = refs[5:]
    size = gram.shape[0]
    blocks = size // BLOCK
    sequences = grads_ref.shape[0]
    bank_chunks, bank_rows, chunk = bank.shape[1:]
    copies = []

    def start(source, target):
        copy = pltpu.make_async_copy(source, target, sems.at[len(copies)])
        copy.start()
        copies.append(copy)

    if halves:
        parts = parts_ref.shape[0]
        span = BLOCK + 8
        me = lax.axis_index("width")
        for i in range(parts):
            for j in range(parts):
                place = lax.bitwise_xor(me, j) * span
                low, high = min(i, j), max(i, j)
                row = 2 * BLOCK * low + (BLOCK if i > j else 0)
                start(
                    parts_ref.at[i, pl.ds(place, BLOCK), :],
                    gram.at[row : row + BLOCK, 2 * BLOCK * high : 2 * BLOCK * (high + 1)],
                )
                if i == j:
                    start(parts_ref.at[i, pl.ds(place + BLOCK, 8), :], tails.at[i])
            for c in range(bank_chunks):
                first = parts * span + c * bank_rows
                start(parts_ref.at[i, first : first + bank_rows, :], bank.at[i, c])
    else:
        start(prior_ref, gram)
        start(bank_ref, bank)
    grads = grads_ref[...]
    left, right = both_terms(grads, 0)
    on_diagonal = eye_mask()
    for copy in copies:
        copy.wait()
    for q in range(ids_ref.shape[0]):
        part, row = ids_ref[q] // bank_rows, ids_ref[q] % bank_rows
        for c in range(bank_chunks):
            extra[sequences + q : sequences + q + 1, c * chunk : (c + 1) * chunk] = bank[
                part, c, pl.ds(row, 1), :
            ]
    extra[:sequences, :] = grads
    diagonal = jnp.zeros((BLOCK, BLOCK), f32)
    if halves:
        upper = lax.broadcasted_iota(jnp.int32, (BLOCK, BLOCK), 0) <= lax.broadcasted_iota(
            jnp.int32, (BLOCK, BLOCK), 1
        )
        for i in range(parts):
            low = 2 * BLOCK * i
            mid, high = low + BLOCK, low + 2 * BLOCK
            packed = gram[low:mid, low:mid]
            turned = packed.T
            gram[low:mid, low:mid] = jnp.where(upper, packed, turned)
            second = jnp.where(
                on_diagonal, tails[i, 0:1, :BLOCK], jnp.where(upper, turned, packed)
            )
            gram[mid:high, mid:high] = second
            diagonal = diagonal + jnp.where(on_diagonal, packed + second, 0.0)
    else:
        for low in range(0, size, BLOCK):
            diagonal = diagonal + jnp.where(
                on_diagonal, gram[low : low + BLOCK, low : low + BLOCK], 0.0
            )
    trace = jnp.sum(diagonal) + jnp.sum(grads * grads) / sequences
    damping = damping_ratio * trace / size
    for low in range(0, size, BLOCK):
        high = low + BLOCK
        product = contract(left[:, low:high], right[:, low:], 0, 0) / sequences
        gram[low:high, low:high] = (
            gram[low:high, low:high]
            + product[:, :BLOCK]
            + jnp.where(on_diagonal, damping, 0.0)
        )
        if high < size:
            gram[low:high, high:] = gram[low:high, high:] + product[:, BLOCK:]
    scores = jnp.zeros((ids_ref.shape[0], sequences), f32)
    for k in range(blocks):
        low, high = k * BLOCK, (k + 1) * BLOCK
        work[:, :BLOCK] = gram[low:high, low:high]
        factor_block(work)
        inverse_left, inverse_right = both_terms(work[:, BLOCK:], 1)
        solved = contract(left_terms(extra[:, low:high], 1), inverse_right, 1, 1)
        solved_left, solved_right = both_terms(solved, 1)
        scores = scores + contract(solved_left[sequences:], solved_right[:sequences], 1, 1)
        if k == blocks - 1:
            break
        panel = contract(inverse_left, right_terms(gram[low:high, high:], 0), 1, 0)
        panel_left, panel_right = both_terms(panel, 0)
        left_ref[:, high:] = panel_left
        right_ref[:, high:] = panel_right
        extra[:, high:] = extra[:, high:] - contract(solved_left, panel_right, 1, 0)
        for i in range(high, size, BLOCK):
            gram[i : i + BLOCK, i:] = gram[i : i + BLOCK, i:] - contract(
                left_ref[:, i : i + BLOCK], right_ref[:, i:], 0, 0
            )
    out_ref[...] = jnp.dot(scores, choose_ref[...], precision=highest)


def solve(halves, ids, prior_operands, bank_shape, grads, choose):
    sequences, size = grads.shape
    rows = sequences + ids.shape[0]
    copies = 1 + bank_shape[0] * (bank_shape[0] + 1 + bank_shape[1])
    vmem = pl.BlockSpec(memory_space=pltpu.VMEM)
    scratch = [
        pltpu.VMEM((size, size), f32),
        pltpu.VMEM((rows, size), f32),
        pltpu.VMEM((BLOCK, 2 * BLOCK), f32),
        pltpu.VMEM((TERMS * BLOCK, size), jnp.bfloat16),
        pltpu.VMEM((TERMS * BLOCK, size), jnp.bfloat16),
    ]
    if halves:
        scratch.append(pltpu.VMEM((bank_shape[0], 8, 2 * BLOCK), f32))
    return pl.pallas_call(
        functools.partial(solve_kernel, halves),
        out_shape=jax.ShapeDtypeStruct((ids.shape[0], choose.shape[1]), f32),
        in_specs=[pl.BlockSpec(memory_space=pltpu.SMEM)]
        + [pl.BlockSpec(memory_space=pl.ANY)] * len(prior_operands)
        + [vmem, vmem],
        out_specs=vmem,
        scratch_shapes=scratch
        + [pltpu.VMEM(bank_shape, f32), pltpu.SemaphoreType.DMA((copies,))],
        compiler_params=pltpu.CompilerParams(vmem_limit_bytes=48 * 2**20),
        cost_estimate=pl.CostEstimate(
            flops=4 * size**3, bytes_accessed=4 * size * size, transcendentals=size
        ),
    )(ids, *prior_operands, grads, choose)


def local(
    layer_inputs,
    output_grads,
    proj_in,
    proj_out,
    prior_gram,
    query_bank,
    slab_sequence,
    seq_lengths,
    query_ids,
):
    width_count = lax.axis_size("width")
    token_count = lax.axis_size("tokens")
    width_index = lax.axis_index("width")
    token_index = lax.axis_index("tokens")
    slab_count = layer_inputs.shape[0] // SEQ_LEN
    sequence_count = slab_sequence.shape[0]
    bank_rows = query_bank.shape[0]
    halves = prior_gram.shape == (2 * BLOCK, 2 * BLOCK)

    if halves:
        pieces = exchange(half_payload(prior_gram, token_index, width_index), "width")
        chunks = query_bank.shape[1] // (2 * BLOCK)
        pieces += [query_bank[:, c * 2 * BLOCK : (c + 1) * 2 * BLOCK] for c in range(chunks)]
        prior_operands = (lax.all_gather(jnp.concatenate(pieces, 0), "tokens", axis=0),)
        bank_shape = (token_count, chunks, bank_rows, 2 * BLOCK)
    else:
        prior_block = lax.all_gather(prior_gram, "width", axis=1, tiled=True)
        prior_full = lax.all_gather(prior_block, "tokens", axis=0, tiled=True)
        bank_shape = (token_count, 1, bank_rows, query_bank.shape[1])
        bank_full = lax.all_gather(query_bank, "tokens", axis=0, tiled=True)
        prior_operands = (prior_full, bank_full.reshape(bank_shape))

    features = (((1,), (1,)), ((), ()))
    projected = jnp.concatenate(
        [
            lax.dot_general(proj_in, layer_inputs, features, preferred_element_type=f32),
            lax.dot_general(proj_out, output_grads, features, preferred_element_type=f32),
        ],
        axis=0,
    )
    total = sum(exchange(projected, "width"))
    local_slabs = lax.dynamic_slice_in_dim(slab_sequence, token_index * slab_count, slab_count)
    seq_numbers = jnp.arange(sequence_count, dtype=jnp.int32)
    local_lengths = jnp.sum(
        jnp.where(local_slabs[:, None] == seq_numbers[None, :], seq_lengths[None, :], 0), axis=1
    )
    offset = jnp.arange(SEQ_LEN, dtype=jnp.int32)
    valid = (offset[None, :] < local_lengths[:, None]).reshape(1, -1)
    total_in = jnp.where(valid, total[:R_IN], 0.0).reshape(R_IN, slab_count, SEQ_LEN)
    total_out = total[R_IN:].reshape(-1, slab_count, SEQ_LEN)
    vectors = lax.dot_general(
        total_in, total_out, (((2,), (2,)), ((1,), (1,))), precision=highest
    ).reshape(slab_count, K)
    all_grads = lax.all_gather(vectors, "tokens", axis=0, tiled=True)

    column_count = sequence_count // width_count
    column_ids = width_index * column_count + jnp.arange(column_count, dtype=jnp.int32)
    choose = (slab_sequence[:, None] == column_ids[None, :]).astype(f32)
    query_count = query_ids.shape[0] // token_count
    local_ids = lax.dynamic_slice_in_dim(query_ids, token_index * query_count, query_count)
    return solve(halves, local_ids, prior_operands, bank_shape, all_grads, choose)


def solution(mesh):
    return jax.shard_map(
        local,
        mesh=mesh,
        in_specs=(
            P(("groups", "tokens"), "width"),
            P(("groups", "tokens"), "width"),
            P(None, "width"),
            P(None, "width"),
            P(("groups", "tokens"), "width"),
            P(("groups", "tokens"), None),
            P("groups"),
            P("groups"),
            P("groups"),
        ),
        out_specs=P(("groups", "tokens"), "width"),
        check_vma=False,
    )
```

```python
import functools

import jax
import jax.numpy as jnp
from jax import lax
from jax.experimental import pallas as pl
from jax.experimental.pallas import tpu as pltpu
from jax.sharding import PartitionSpec as P

R_IN = 32
SEQ_LEN = 128
K = 1024
BLOCK = 128
PIVOTS = 16
TERMS = 6
f32 = jnp.float32


damping_ratio = 0.1
highest = lax.Precision.HIGHEST


def split_terms(value):
    high = value.astype(jnp.bfloat16)
    rest = value - high.astype(f32)
    mid = rest.astype(jnp.bfloat16)
    low = (rest - mid.astype(f32)).astype(jnp.bfloat16)
    return high, mid, low


def left_terms(value, axis):
    high, mid, low = split_terms(value)
    return jnp.concatenate([high, high, mid, mid, high, low], axis)


def right_terms(value, axis):
    high, mid, low = split_terms(value)
    return jnp.concatenate([high, mid, high, mid, low, high], axis)


def both_terms(value, axis):
    high, mid, low = split_terms(value)
    return (
        jnp.concatenate([high, high, mid, mid, high, low], axis),
        jnp.concatenate([high, mid, high, mid, low, high], axis),
    )


def contract(a, b, a_dim, b_dim):
    return lax.dot_general(a, b, (((a_dim,), (b_dim,)), ((), ())), preferred_element_type=f32)


def eye_mask():
    shape = (BLOCK, BLOCK)
    return lax.broadcasted_iota(jnp.int32, shape, 0) == lax.broadcasted_iota(jnp.int32, shape, 1)


def factor_block(work):
    work[:, BLOCK:] = eye_mask().astype(f32)
    tiles = PIVOTS // 8
    row = lax.broadcasted_iota(jnp.int32, (8, 2 * BLOCK), 0)
    for group in range(BLOCK // PIVOTS):
        base = group * PIVOTS
        rows = [work[base + 8 * h : base + 8 * h + 8, :] for h in range(tiles)]
        columns = [
            [
                jnp.broadcast_to(
                    work[base + 8 * h : base + 8 * h + 8, base + j : base + j + 1], (8, BLOCK)
                )
                for h in range(tiles)
            ]
            for j in range(PIVOTS)
        ]
        for j in range(PIVOTS):
            hj, jj = divmod(j, 8)
            scale = lax.rsqrt(jnp.broadcast_to(columns[j][hj][jj : jj + 1, :], (8, BLOCK)))
            lower = [columns[j][h] * scale for h in range(hj, tiles)]
            pivot_row = jnp.broadcast_to(rows[hj][jj : jj + 1, :], (8, 2 * BLOCK)) * jnp.concatenate(
                [scale, scale], 1
            )
            for l in range(j + 1, PIVOTS):
                entry = jnp.broadcast_to(columns[l][hj][jj : jj + 1, :], (8, BLOCK)) * scale
                for h in range(hj, tiles):
                    columns[l][h] = columns[l][h] - lower[h - hj] * entry
            for h in range(hj, tiles):
                wide = jnp.concatenate([lower[h - hj], lower[h - hj]], 1)
                changed = rows[h] - wide * pivot_row
                if h == hj:
                    changed = jnp.where(
                        row > jj, changed, jnp.where(row == jj, pivot_row, rows[h])
                    )
                rows[h] = changed
        done = jnp.concatenate(rows, 0)
        work[base : base + PIVOTS, :] = done
        if base + PIVOTS < BLOCK:
            left, right = both_terms(done, 0)
            change = contract(left[:, :BLOCK], right, 0, 0)
            work[base + PIVOTS :, :] = work[base + PIVOTS :, :] - change[base + PIVOTS :, :]


def pack_kernel(prior_ref, bank_ref, half_ref, first_ref):
    row_part, col_part = lax.axis_index("tokens"), lax.axis_index("width")
    on_diagonal = eye_mask()

    def put(rows, columns, value):
        half_ref[rows, columns] = value
        first_ref[rows, columns] = value

    top, left, right = slice(0, BLOCK), slice(0, BLOCK), slice(BLOCK, 2 * BLOCK)

    @pl.when(row_part == col_part)
    def _():
        shape = (BLOCK, BLOCK)
        upper = lax.broadcasted_iota(jnp.int32, shape, 0) <= lax.broadcasted_iota(
            jnp.int32, shape, 1
        )
        put(top, left, jnp.where(upper, prior_ref[:BLOCK, :BLOCK], prior_ref[BLOCK:, BLOCK:]))
        put(top, right, prior_ref[:BLOCK, BLOCK:])

    @pl.when(row_part < col_part)
    def _():
        put(top, slice(None), prior_ref[:BLOCK, :])

    @pl.when(row_part > col_part)
    def _():
        put(top, left, prior_ref[:BLOCK, BLOCK:].T)
        put(top, right, prior_ref[BLOCK:, BLOCK:].T)

    diagonal = jnp.sum(jnp.where(on_diagonal, prior_ref[BLOCK:, BLOCK:], 0.0), axis=0, keepdims=True)
    tail = slice(BLOCK, BLOCK + 8)
    put(tail, left, jnp.broadcast_to(diagonal, (8, BLOCK)))
    put(tail, right, jnp.zeros((8, BLOCK), f32))
    bank_rows = bank_ref.shape[0]
    for c in range(bank_ref.shape[1] // (2 * BLOCK)):
        low = BLOCK + 8 + c * bank_rows
        first_ref[low : low + bank_rows, :] = bank_ref[:, c * 2 * BLOCK : (c + 1) * 2 * BLOCK]


def pack(prior, bank):
    span = BLOCK + 8
    rows = span + bank.size // (2 * BLOCK)
    vmem = pl.BlockSpec(memory_space=pltpu.VMEM)
    return pl.pallas_call(
        pack_kernel,
        out_shape=(
            jax.ShapeDtypeStruct((span, 2 * BLOCK), f32),
            jax.ShapeDtypeStruct((rows, 2 * BLOCK), f32),
        ),
        in_specs=[vmem, vmem],
        out_specs=(vmem, vmem),
    )(prior, bank)


def exchange(value, axis):
    count = lax.axis_size(axis)
    return [value] + [
        lax.ppermute(value, axis, [(i, i ^ s) for i in range(count)]) for s in range(1, count)
    ]


def solve_kernel(halves, ids_ref, *refs):
    if halves:
        own_ref, others_ref, grads_ref, choose_ref, out_ref = refs[:5]
        gram, extra, work, left_ref, right_ref, tails, bank, sems = refs[5:]
    else:
        prior_ref, bank_ref, grads_ref, choose_ref, out_ref = refs[:5]
        gram, extra, work, left_ref, right_ref, bank, sems = refs[5:]
    size = gram.shape[0]
    blocks = size // BLOCK
    sequences = grads_ref.shape[0]
    bank_chunks, bank_rows, chunk = bank.shape[1:]
    copies = []

    def start(source, target):
        copy = pltpu.make_async_copy(source, target, sems.at[len(copies)])
        copy.start()
        copies.append(copy)

    if halves:
        parts = own_ref.shape[0]
        span = BLOCK + 8
        me = lax.axis_index("width")
        for s in range(parts):
            j = lax.bitwise_xor(me, s)
            source, place = (own_ref, 0) if s == 0 else (others_ref, (s - 1) * span)
            for i in range(parts):
                row = 2 * BLOCK * lax.min(i, j) + jnp.where(i > j, BLOCK, 0)
                row = pl.multiple_of(row, BLOCK)
                column = pl.multiple_of(2 * BLOCK * lax.max(i, j), BLOCK)
                start(
                    source.at[i, place : place + BLOCK, :],
                    gram.at[pl.ds(row, BLOCK), pl.ds(column, 2 * BLOCK)],
                )
                start(source.at[i, place + BLOCK : place + span, :], tails.at[i, j])
        for i in range(parts):
            for c in range(bank_chunks):
                first = span + c * bank_rows
                start(own_ref.at[i, first : first + bank_rows, :], bank.at[i, c])
    else:
        start(prior_ref, gram)
        start(bank_ref, bank)
    grads = grads_ref[...]
    left, right = both_terms(grads, 0)
    on_diagonal = eye_mask()
    for copy in copies:
        copy.wait()
    for q in range(ids_ref.shape[0]):
        part, row = ids_ref[q] // bank_rows, ids_ref[q] % bank_rows
        for c in range(bank_chunks):
            extra[sequences + q : sequences + q + 1, c * chunk : (c + 1) * chunk] = bank[
                part, c, pl.ds(row, 1), :
            ]
    extra[:sequences, :] = grads
    diagonal = jnp.zeros((BLOCK, BLOCK), f32)
    if halves:
        upper = lax.broadcasted_iota(jnp.int32, (BLOCK, BLOCK), 0) <= lax.broadcasted_iota(
            jnp.int32, (BLOCK, BLOCK), 1
        )
        for i in range(parts):
            low = 2 * BLOCK * i
            mid, high = low + BLOCK, low + 2 * BLOCK
            packed = gram[low:mid, low:mid]
            turned = packed.T
            gram[low:mid, low:mid] = jnp.where(upper, packed, turned)
            second = jnp.where(
                on_diagonal, tails[i, i, 0:1, :BLOCK], jnp.where(upper, turned, packed)
            )
            gram[mid:high, mid:high] = second
            diagonal = diagonal + jnp.where(on_diagonal, packed + second, 0.0)
    else:
        for low in range(0, size, BLOCK):
            diagonal = diagonal + jnp.where(
                on_diagonal, gram[low : low + BLOCK, low : low + BLOCK], 0.0
            )
    trace = jnp.sum(diagonal) + jnp.sum(grads * grads) / sequences
    damping = damping_ratio * trace / size
    for low in range(0, size, BLOCK):
        high = low + BLOCK
        product = contract(left[:, low:high], right[:, low:], 0, 0) / sequences
        gram[low:high, low:high] = (
            gram[low:high, low:high]
            + product[:, :BLOCK]
            + jnp.where(on_diagonal, damping, 0.0)
        )
        if high < size:
            gram[low:high, high:] = gram[low:high, high:] + product[:, BLOCK:]
    scores = jnp.zeros((ids_ref.shape[0], sequences), f32)
    for k in range(blocks):
        low, high = k * BLOCK, (k + 1) * BLOCK
        work[:, :BLOCK] = gram[low:high, low:high]
        factor_block(work)
        inverse_left, inverse_right = both_terms(work[:, BLOCK:], 1)
        solved = contract(left_terms(extra[:, low:high], 1), inverse_right, 1, 1)
        solved_left, solved_right = both_terms(solved, 1)
        scores = scores + contract(solved_left[sequences:], solved_right[:sequences], 1, 1)
        if k == blocks - 1:
            break
        panel = contract(inverse_left, right_terms(gram[low:high, high:], 0), 1, 0)
        panel_left, panel_right = both_terms(panel, 0)
        left_ref[:, high:] = panel_left
        right_ref[:, high:] = panel_right
        extra[:, high:] = extra[:, high:] - contract(solved_left, panel_right, 1, 0)
        for i in range(high, size, BLOCK):
            gram[i : i + BLOCK, i:] = gram[i : i + BLOCK, i:] - contract(
                left_ref[:, i : i + BLOCK], right_ref[:, i:], 0, 0
            )
    out_ref[...] = lax.dot_general(
        choose_ref[...], scores, (((1,), (1,)), ((), ())), precision=highest
    )


def solve(halves, ids, prior_operands, bank_shape, grads, choose):
    sequences, size = grads.shape
    rows = sequences + ids.shape[0]
    copies = 2 + bank_shape[0] * (2 * bank_shape[0] + bank_shape[1])
    vmem = pl.BlockSpec(memory_space=pltpu.VMEM)
    scratch = [
        pltpu.VMEM((size, size), f32),
        pltpu.VMEM((rows, size), f32),
        pltpu.VMEM((BLOCK, 2 * BLOCK), f32),
        pltpu.VMEM((TERMS * BLOCK, size), jnp.bfloat16),
        pltpu.VMEM((TERMS * BLOCK, size), jnp.bfloat16),
    ]
    if halves:
        scratch.append(pltpu.VMEM((bank_shape[0], bank_shape[0], 8, 2 * BLOCK), f32))
    return pl.pallas_call(
        functools.partial(solve_kernel, halves),
        out_shape=jax.ShapeDtypeStruct((choose.shape[0], ids.shape[0]), f32),
        in_specs=[pl.BlockSpec(memory_space=pltpu.SMEM)]
        + [pl.BlockSpec(memory_space=pl.ANY)] * len(prior_operands)
        + [vmem, vmem],
        out_specs=vmem,
        scratch_shapes=scratch
        + [pltpu.VMEM(bank_shape, f32), pltpu.SemaphoreType.DMA((copies,))],
        compiler_params=pltpu.CompilerParams(vmem_limit_bytes=60 * 2**20),
        cost_estimate=pl.CostEstimate(
            flops=4 * size**3, bytes_accessed=4 * size * size, transcendentals=size
        ),
    )(ids, *prior_operands, grads, choose)


def local(
    layer_inputs,
    output_grads,
    proj_in,
    proj_out,
    prior_gram,
    query_bank,
    slab_sequence,
    seq_lengths,
    query_ids,
):
    width_count = lax.axis_size("width")
    token_count = lax.axis_size("tokens")
    width_index = lax.axis_index("width")
    token_index = lax.axis_index("tokens")
    slab_count = layer_inputs.shape[0] // SEQ_LEN
    sequence_count = slab_sequence.shape[0]
    bank_rows = query_bank.shape[0]
    halves = prior_gram.shape == (2 * BLOCK, 2 * BLOCK)

    if halves:
        half, first = pack(prior_gram, query_bank)
        own = lax.all_gather(first, "tokens", axis=0)
        pieces = exchange(half, "width")[1:]
        bank_shape = (token_count, query_bank.shape[1] // (2 * BLOCK), bank_rows, 2 * BLOCK)
    else:
        prior_block = lax.all_gather(prior_gram, "width", axis=1, tiled=True)
        prior_full = lax.all_gather(prior_block, "tokens", axis=0, tiled=True)
        bank_shape = (token_count, 1, bank_rows, query_bank.shape[1])
        bank_full = lax.all_gather(query_bank, "tokens", axis=0, tiled=True)
        prior_operands = (prior_full, bank_full.reshape(bank_shape))

    features = (((1,), (1,)), ((), ()))
    projected = jnp.concatenate(
        [
            lax.dot_general(proj_in, layer_inputs, features, preferred_element_type=f32),
            lax.dot_general(proj_out, output_grads, features, preferred_element_type=f32),
        ],
        axis=0,
    )
    if halves:
        projected, pieces = lax.optimization_barrier((projected, pieces))
        others = lax.all_gather(jnp.concatenate(pieces, 0), "tokens", axis=0)
        prior_operands = (own, others)
    total = sum(exchange(projected, "width"))
    local_slabs = lax.dynamic_slice_in_dim(slab_sequence, token_index * slab_count, slab_count)
    seq_numbers = jnp.arange(sequence_count, dtype=jnp.int32)
    local_lengths = jnp.sum(
        jnp.where(local_slabs[:, None] == seq_numbers[None, :], seq_lengths[None, :], 0), axis=1
    )
    offset = jnp.arange(SEQ_LEN, dtype=jnp.int32)
    valid = (offset[None, :] < local_lengths[:, None]).reshape(1, -1)
    total_in = jnp.where(valid, total[:R_IN], 0.0).reshape(R_IN, slab_count, SEQ_LEN)
    total_out = total[R_IN:].reshape(-1, slab_count, SEQ_LEN)
    vectors = lax.dot_general(
        total_in, total_out, (((2,), (2,)), ((1,), (1,))), precision=highest
    ).reshape(slab_count, K)
    all_grads = lax.all_gather(vectors, "tokens", axis=0, tiled=True)

    column_count = sequence_count // width_count
    column_ids = width_index * column_count + jnp.arange(column_count, dtype=jnp.int32)
    choose = (column_ids[:, None] == slab_sequence[None, :]).astype(f32)
    query_count = query_ids.shape[0] // token_count
    local_ids = lax.dynamic_slice_in_dim(query_ids, token_index * query_count, query_count)
    return solve(halves, local_ids, prior_operands, bank_shape, all_grads, choose).T


def solution(mesh):
    return jax.shard_map(
        local,
        mesh=mesh,
        in_specs=(
            P(("groups", "tokens"), "width"),
            P(("groups", "tokens"), "width"),
            P(None, "width"),
            P(None, "width"),
            P(("groups", "tokens"), "width"),
            P(("groups", "tokens"), None),
            P("groups"),
            P("groups"),
            P("groups"),
        ),
        out_specs=P(("groups", "tokens"), "width"),
        check_vma=False,
    )
```

```python
import functools

import jax
import jax.numpy as jnp
from jax import lax
from jax.experimental import pallas as pl
from jax.experimental.pallas import tpu as pltpu
from jax.sharding import PartitionSpec as P

R_IN = 32
SEQ_LEN = 128
K = 1024
BLOCK = 128
PIVOTS = 16
WINDOW = 32
TERMS = 6
f32 = jnp.float32


damping_ratio = 0.1
highest = lax.Precision.HIGHEST


def split_terms(value):
    high = value.astype(jnp.bfloat16)
    rest = value - high.astype(f32)
    mid = rest.astype(jnp.bfloat16)
    low = (rest - mid.astype(f32)).astype(jnp.bfloat16)
    return high, mid, low


def left_terms(value, axis):
    high, mid, low = split_terms(value)
    return jnp.concatenate([high, high, mid, mid, high, low], axis)


def right_terms(value, axis):
    high, mid, low = split_terms(value)
    return jnp.concatenate([high, mid, high, mid, low, high], axis)


def both_terms(value, axis):
    high, mid, low = split_terms(value)
    return (
        jnp.concatenate([high, high, mid, mid, high, low], axis),
        jnp.concatenate([high, mid, high, mid, low, high], axis),
    )


def contract(a, b, a_dim, b_dim):
    return lax.dot_general(a, b, (((a_dim,), (b_dim,)), ((), ())), preferred_element_type=f32)


def eye_mask():
    shape = (BLOCK, BLOCK)
    return lax.broadcasted_iota(jnp.int32, shape, 0) == lax.broadcasted_iota(jnp.int32, shape, 1)


def factor_block(work, pending):
    row = lax.broadcasted_iota(jnp.int32, (8, BLOCK), 0)
    lane = lax.broadcasted_iota(jnp.int32, (8, BLOCK), 1)
    tiles = WINDOW // 8
    for base in range(0, BLOCK, WINDOW):
        rows = [work[base + 8 * h : base + 8 * h + 8, :] for h in range(tiles)]
        for group in range(0, WINDOW, PIVOTS):
            columns = [
                {
                    h: jnp.broadcast_to(rows[h][:, column : column + 1], (8, BLOCK))
                    for h in range(group // 8, tiles)
                }
                for column in range(base + group, base + group + PIVOTS)
            ]
            pending()
            for j in range(PIVOTS):
                hj, jj = divmod(group + j, 8)
                here = lane == base + group + j
                scale = lax.rsqrt(jnp.broadcast_to(columns[j][hj][jj : jj + 1, :], (8, BLOCK)))
                lower = {h: columns[j][h] * scale for h in range(hj, tiles)}
                for l in range(j + 1, PIVOTS):
                    entry = jnp.broadcast_to(columns[l][hj][jj : jj + 1, :], (8, BLOCK)) * scale
                    for h in range(hj, tiles):
                        columns[l][h] = columns[l][h] - lower[h] * entry
                pivot_row = jnp.broadcast_to(rows[hj][jj : jj + 1, :], (8, BLOCK))
                pivot_row = jnp.where(here, 1.0, pivot_row) * scale
                for h in range(hj, tiles):
                    changed = jnp.where(here, 0.0, rows[h]) - lower[h] * pivot_row
                    if h == hj:
                        changed = jnp.where(
                            row > jj, changed, jnp.where(row == jj, pivot_row, rows[h])
                        )
                    rows[h] = changed
        done = jnp.concatenate(rows, 0)
        end = base + WINDOW
        work[base:end, :] = done
        if end < BLOCK:
            window_row = base + lax.broadcasted_iota(jnp.int32, (WINDOW, BLOCK), 0)
            window_lane = lax.broadcasted_iota(jnp.int32, (WINDOW, BLOCK), 1)
            above = (window_lane > window_row) & (window_lane < end)
            change = contract(
                left_terms(done, 0), right_terms(jnp.where(above, 0.0, done), 0), 0, 0
            )
            rest_lane = lax.broadcasted_iota(jnp.int32, (BLOCK - end, BLOCK), 1)
            taken = (rest_lane >= base) & (rest_lane < end)
            work[end:, :] = jnp.where(taken, 0.0, work[end:, :]) - change[end:, :]


def pack_kernel(prior_ref, bank_ref, half_ref, first_ref):
    row_part, col_part = lax.axis_index("tokens"), lax.axis_index("width")
    on_diagonal = eye_mask()

    def put(rows, columns, value):
        half_ref[rows, columns] = value
        first_ref[rows, columns] = value

    top, left, right = slice(0, BLOCK), slice(0, BLOCK), slice(BLOCK, 2 * BLOCK)

    @pl.when(row_part == col_part)
    def _():
        shape = (BLOCK, BLOCK)
        upper = lax.broadcasted_iota(jnp.int32, shape, 0) <= lax.broadcasted_iota(
            jnp.int32, shape, 1
        )
        put(top, left, jnp.where(upper, prior_ref[:BLOCK, :BLOCK], prior_ref[BLOCK:, BLOCK:]))
        put(top, right, prior_ref[:BLOCK, BLOCK:])

    @pl.when(row_part < col_part)
    def _():
        put(top, slice(None), prior_ref[:BLOCK, :])

    @pl.when(row_part > col_part)
    def _():
        put(top, left, prior_ref[:BLOCK, BLOCK:].T)
        put(top, right, prior_ref[BLOCK:, BLOCK:].T)

    diagonal = jnp.sum(jnp.where(on_diagonal, prior_ref[BLOCK:, BLOCK:], 0.0), axis=0, keepdims=True)
    tail = slice(BLOCK, BLOCK + 8)
    put(tail, left, jnp.broadcast_to(diagonal, (8, BLOCK)))
    put(tail, right, jnp.zeros((8, BLOCK), f32))
    bank_rows = bank_ref.shape[0]
    for c in range(bank_ref.shape[1] // (2 * BLOCK)):
        low = BLOCK + 8 + c * bank_rows
        first_ref[low : low + bank_rows, :] = bank_ref[:, c * 2 * BLOCK : (c + 1) * 2 * BLOCK]


def pack(prior, bank):
    span = BLOCK + 8
    rows = span + bank.size // (2 * BLOCK)
    vmem = pl.BlockSpec(memory_space=pltpu.VMEM)
    return pl.pallas_call(
        pack_kernel,
        out_shape=(
            jax.ShapeDtypeStruct((span, 2 * BLOCK), f32),
            jax.ShapeDtypeStruct((rows, 2 * BLOCK), f32),
        ),
        in_specs=[vmem, vmem],
        out_specs=(vmem, vmem),
    )(prior, bank)


def exchange(value, axis):
    count = lax.axis_size(axis)
    return [value] + [
        lax.ppermute(value, axis, [(i, i ^ s) for i in range(count)]) for s in range(1, count)
    ]


def solve_kernel(halves, ids_ref, *refs):
    if halves:
        own_ref, others_ref, grads_ref, choose_ref, out_ref = refs[:5]
        gram, extra, work, left_ref, right_ref, tails, bank, sems = refs[5:]
    else:
        prior_ref, bank_ref, grads_ref, choose_ref, out_ref = refs[:5]
        gram, extra, work, left_ref, right_ref, bank, sems = refs[5:]
    size = gram.shape[0]
    blocks = size // BLOCK
    sequences = grads_ref.shape[0]
    bank_chunks, bank_rows, chunk = bank.shape[1:]
    copies = []

    def start(source, target):
        copy = pltpu.make_async_copy(source, target, sems.at[len(copies)])
        copy.start()
        copies.append(copy)

    if halves:
        parts = own_ref.shape[0]
        span = BLOCK + 8
        me = lax.axis_index("width")
        for s in range(parts):
            j = lax.bitwise_xor(me, s)
            source, place = (own_ref, 0) if s == 0 else (others_ref, (s - 1) * span)
            for i in range(parts):
                row = 2 * BLOCK * lax.min(i, j) + jnp.where(i > j, BLOCK, 0)
                row = pl.multiple_of(row, BLOCK)
                column = pl.multiple_of(2 * BLOCK * lax.max(i, j), BLOCK)
                start(
                    source.at[i, place : place + BLOCK, :],
                    gram.at[pl.ds(row, BLOCK), pl.ds(column, 2 * BLOCK)],
                )
                start(source.at[i, place + BLOCK : place + span, :], tails.at[i, j])
        for i in range(parts):
            for c in range(bank_chunks):
                first = span + c * bank_rows
                start(own_ref.at[i, first : first + bank_rows, :], bank.at[i, c])
    else:
        start(prior_ref, gram)
        start(bank_ref, bank)
    grads = grads_ref[...]
    left, right = both_terms(grads, 0)
    on_diagonal = eye_mask()
    for copy in copies:
        copy.wait()
    for q in range(ids_ref.shape[0]):
        part, row = ids_ref[q] // bank_rows, ids_ref[q] % bank_rows
        for c in range(bank_chunks):
            extra[sequences + q : sequences + q + 1, c * chunk : (c + 1) * chunk] = bank[
                part, c, pl.ds(row, 1), :
            ]
    extra[:sequences, :] = grads
    diagonal = jnp.zeros((BLOCK, BLOCK), f32)
    if halves:
        upper = lax.broadcasted_iota(jnp.int32, (BLOCK, BLOCK), 0) <= lax.broadcasted_iota(
            jnp.int32, (BLOCK, BLOCK), 1
        )
        for i in range(parts):
            low = 2 * BLOCK * i
            mid, high = low + BLOCK, low + 2 * BLOCK
            packed = gram[low:mid, low:mid]
            turned = packed.T
            gram[low:mid, low:mid] = jnp.where(upper, packed, turned)
            second = jnp.where(
                on_diagonal, tails[i, i, 0:1, :BLOCK], jnp.where(upper, turned, packed)
            )
            gram[mid:high, mid:high] = second
            diagonal = diagonal + jnp.where(on_diagonal, packed + second, 0.0)
    else:
        for low in range(0, size, BLOCK):
            diagonal = diagonal + jnp.where(
                on_diagonal, gram[low : low + BLOCK, low : low + BLOCK], 0.0
            )
    trace = jnp.sum(diagonal) + jnp.sum(grads * grads) / sequences
    damping = damping_ratio * trace / size
    for low in range(0, size, BLOCK):
        high = low + BLOCK
        product = contract(left[:, low:high], right[:, low:], 0, 0) / sequences
        gram[low:high, low:high] = (
            gram[low:high, low:high]
            + product[:, :BLOCK]
            + jnp.where(on_diagonal, damping, 0.0)
        )
        if high < size:
            gram[low:high, high:] = gram[low:high, high:] + product[:, BLOCK:]
    scores = [jnp.zeros((ids_ref.shape[0], sequences), f32)]
    lower = lax.broadcasted_iota(jnp.int32, (BLOCK, BLOCK), 0) >= lax.broadcasted_iota(
        jnp.int32, (BLOCK, BLOCK), 1
    )
    waiting = []

    def pending():
        if waiting:
            waiting.pop(0)()

    def panel(inverse_left, block, low, high):
        left, right = both_terms(
            contract(inverse_left, right_terms(gram[block : block + BLOCK, low:high], 0), 1, 0), 0
        )
        left_ref[:, low:high] = left
        right_ref[:, low:high] = right
        return left, right

    def update(row, low):
        gram[row : row + BLOCK, low:] = gram[row : row + BLOCK, low:] - contract(
            left_ref[:, row : row + BLOCK], right_ref[:, low:], 0, 0
        )

    def update_extra(inverse_right, low, high):
        solved = contract(left_terms(extra[:, low:high], 1), inverse_right, 1, 1)
        solved_left, solved_right = both_terms(solved, 1)
        scores[0] = scores[0] + contract(solved_left[sequences:], solved_right[:sequences], 1, 1)
        if high < size:
            extra[:, high:] = extra[:, high:] - contract(solved_left, right_ref[:, high:], 1, 0)

    for low in range(0, size, BLOCK):
        high = low + BLOCK
        work[...] = gram[low:high, low:high]
        factor_block(work, pending)
        while waiting:
            pending()
        inverse_left, inverse_right = both_terms(jnp.where(lower, work[...], 0.0), 1)
        if high < size:
            after = high + BLOCK
            left, right = panel(inverse_left, low, high, after)
            gram[high:after, high:after] = gram[high:after, high:after] - contract(
                left, right, 0, 0
            )
            if after < size:
                middle = after + ((size - after) // BLOCK + 1) // 2 * BLOCK
                waiting.append(functools.partial(panel, inverse_left, low, after, middle))
                if middle < size:
                    waiting.append(functools.partial(panel, inverse_left, low, middle, size))
                waiting.append(functools.partial(update, high, after))
        waiting.append(functools.partial(update_extra, inverse_right, low, high))
        for row in range(high + BLOCK, size, BLOCK):
            waiting.append(functools.partial(update, row, row))
    while waiting:
        pending()
    out_ref[...] = lax.dot_general(
        choose_ref[...], scores[0], (((1,), (1,)), ((), ())), precision=highest
    )


def solve(halves, ids, prior_operands, bank_shape, grads, choose):
    sequences, size = grads.shape
    rows = sequences + ids.shape[0]
    copies = 2 + bank_shape[0] * (2 * bank_shape[0] + bank_shape[1])
    vmem = pl.BlockSpec(memory_space=pltpu.VMEM)
    scratch = [
        pltpu.VMEM((size, size), f32),
        pltpu.VMEM((rows, size), f32),
        pltpu.VMEM((BLOCK, BLOCK), f32),
        pltpu.VMEM((TERMS * BLOCK, size), jnp.bfloat16),
        pltpu.VMEM((TERMS * BLOCK, size), jnp.bfloat16),
    ]
    if halves:
        scratch.append(pltpu.VMEM((bank_shape[0], bank_shape[0], 8, 2 * BLOCK), f32))
    return pl.pallas_call(
        functools.partial(solve_kernel, halves),
        out_shape=jax.ShapeDtypeStruct((choose.shape[0], ids.shape[0]), f32),
        in_specs=[pl.BlockSpec(memory_space=pltpu.SMEM)]
        + [pl.BlockSpec(memory_space=pl.ANY)] * len(prior_operands)
        + [vmem, vmem],
        out_specs=vmem,
        scratch_shapes=scratch
        + [pltpu.VMEM(bank_shape, f32), pltpu.SemaphoreType.DMA((copies,))],
        compiler_params=pltpu.CompilerParams(vmem_limit_bytes=60 * 2**20),
        cost_estimate=pl.CostEstimate(
            flops=4 * size**3, bytes_accessed=4 * size * size, transcendentals=size
        ),
    )(ids, *prior_operands, grads, choose)


def local(
    layer_inputs,
    output_grads,
    proj_in,
    proj_out,
    prior_gram,
    query_bank,
    slab_sequence,
    seq_lengths,
    query_ids,
):
    width_count = lax.axis_size("width")
    token_count = lax.axis_size("tokens")
    width_index = lax.axis_index("width")
    token_index = lax.axis_index("tokens")
    slab_count = layer_inputs.shape[0] // SEQ_LEN
    sequence_count = slab_sequence.shape[0]
    bank_rows = query_bank.shape[0]
    halves = prior_gram.shape == (2 * BLOCK, 2 * BLOCK)

    if halves:
        half, first = pack(prior_gram, query_bank)
        own = lax.all_gather(first, "tokens", axis=0)
        pieces = exchange(half, "width")[1:]
        bank_shape = (token_count, query_bank.shape[1] // (2 * BLOCK), bank_rows, 2 * BLOCK)
    else:
        prior_block = lax.all_gather(prior_gram, "width", axis=1, tiled=True)
        prior_full = lax.all_gather(prior_block, "tokens", axis=0, tiled=True)
        bank_shape = (token_count, 1, bank_rows, query_bank.shape[1])
        bank_full = lax.all_gather(query_bank, "tokens", axis=0, tiled=True)
        prior_operands = (prior_full, bank_full.reshape(bank_shape))

    features = (((1,), (1,)), ((), ()))
    projected = jnp.concatenate(
        [
            lax.dot_general(proj_in, layer_inputs, features, preferred_element_type=f32),
            lax.dot_general(proj_out, output_grads, features, preferred_element_type=f32),
        ],
        axis=0,
    )
    if halves:
        projected, pieces = lax.optimization_barrier((projected, pieces))
        others = lax.all_gather(jnp.concatenate(pieces, 0), "tokens", axis=0)
        prior_operands = (own, others)
    total = sum(exchange(projected, "width"))
    local_slabs = lax.dynamic_slice_in_dim(slab_sequence, token_index * slab_count, slab_count)
    seq_numbers = jnp.arange(sequence_count, dtype=jnp.int32)
    local_lengths = jnp.sum(
        jnp.where(local_slabs[:, None] == seq_numbers[None, :], seq_lengths[None, :], 0), axis=1
    )
    offset = jnp.arange(SEQ_LEN, dtype=jnp.int32)
    valid = (offset[None, :] < local_lengths[:, None]).reshape(1, -1)
    total_in = jnp.where(valid, total[:R_IN], 0.0).reshape(R_IN, slab_count, SEQ_LEN)
    total_out = total[R_IN:].reshape(-1, slab_count, SEQ_LEN)
    vectors = lax.dot_general(
        total_in, total_out, (((2,), (2,)), ((1,), (1,))), precision=highest
    ).reshape(slab_count, K)
    all_grads = lax.all_gather(vectors, "tokens", axis=0, tiled=True)

    column_count = sequence_count // width_count
    column_ids = width_index * column_count + jnp.arange(column_count, dtype=jnp.int32)
    choose = (column_ids[:, None] == slab_sequence[None, :]).astype(f32)
    query_count = query_ids.shape[0] // token_count
    local_ids = lax.dynamic_slice_in_dim(query_ids, token_index * query_count, query_count)
    return solve(halves, local_ids, prior_operands, bank_shape, all_grads, choose).T


def solution(mesh):
    return jax.shard_map(
        local,
        mesh=mesh,
        in_specs=(
            P(("groups", "tokens"), "width"),
            P(("groups", "tokens"), "width"),
            P(None, "width"),
            P(None, "width"),
            P(("groups", "tokens"), "width"),
            P(("groups", "tokens"), None),
            P("groups"),
            P("groups"),
            P("groups"),
        ),
        out_specs=P(("groups", "tokens"), "width"),
        check_vma=False,
    )
```

```python
import functools

import jax
import jax.numpy as jnp
from jax import lax
from jax.experimental import pallas as pl
from jax.experimental.pallas import tpu as pltpu
from jax.sharding import PartitionSpec as P

R_IN = 32
SEQ_LEN = 128
K = 1024
BLOCK = 128
PIVOTS = 16
WINDOW = 32
TERMS = 6
f32 = jnp.float32


damping_ratio = 0.1
highest = lax.Precision.HIGHEST


def split_terms(value):
    high = value.astype(jnp.bfloat16)
    rest = value - high.astype(f32)
    mid = rest.astype(jnp.bfloat16)
    low = (rest - mid.astype(f32)).astype(jnp.bfloat16)
    return high, mid, low


def left_terms(value, axis):
    high, mid, low = split_terms(value)
    return jnp.concatenate([high, high, mid, mid, high, low], axis)


def right_terms(value, axis):
    high, mid, low = split_terms(value)
    return jnp.concatenate([high, mid, high, mid, low, high], axis)


def both_terms(value, axis):
    high, mid, low = split_terms(value)
    return (
        jnp.concatenate([high, high, mid, mid, high, low], axis),
        jnp.concatenate([high, mid, high, mid, low, high], axis),
    )


def contract(a, b, a_dim, b_dim):
    return lax.dot_general(a, b, (((a_dim,), (b_dim,)), ((), ())), preferred_element_type=f32)


def eye_mask():
    shape = (BLOCK, BLOCK)
    return lax.broadcasted_iota(jnp.int32, shape, 0) == lax.broadcasted_iota(jnp.int32, shape, 1)


def factor_block(work, pending):
    row = lax.broadcasted_iota(jnp.int32, (8, BLOCK), 0)
    lane = lax.broadcasted_iota(jnp.int32, (8, BLOCK), 1)
    tiles = WINDOW // 8
    for base in range(0, BLOCK, WINDOW):
        rows = [work[base + 8 * h : base + 8 * h + 8, :] for h in range(tiles)]
        for group in range(0, WINDOW, PIVOTS):
            columns = [
                {
                    h: jnp.broadcast_to(rows[h][:, column : column + 1], (8, BLOCK))
                    for h in range(group // 8, tiles)
                }
                for column in range(base + group, base + group + PIVOTS)
            ]
            pending()
            for j in range(PIVOTS):
                hj, jj = divmod(group + j, 8)
                here = lane == base + group + j
                scale = lax.rsqrt(jnp.broadcast_to(columns[j][hj][jj : jj + 1, :], (8, BLOCK)))
                lower = {h: columns[j][h] * scale for h in range(hj, tiles)}
                for l in range(j + 1, PIVOTS):
                    entry = jnp.broadcast_to(columns[l][hj][jj : jj + 1, :], (8, BLOCK)) * scale
                    for h in range(hj, tiles):
                        columns[l][h] = columns[l][h] - lower[h] * entry
                pivot_row = jnp.broadcast_to(rows[hj][jj : jj + 1, :], (8, BLOCK))
                pivot_row = jnp.where(here, 1.0, pivot_row) * scale
                for h in range(hj, tiles):
                    changed = jnp.where(here, 0.0, rows[h]) - lower[h] * pivot_row
                    if h == hj:
                        changed = jnp.where(
                            row > jj, changed, jnp.where(row == jj, pivot_row, rows[h])
                        )
                    rows[h] = changed
        done = jnp.concatenate(rows, 0)
        end = base + WINDOW
        work[base:end, :] = done
        if end < BLOCK:
            window_row = base + lax.broadcasted_iota(jnp.int32, (WINDOW, BLOCK), 0)
            window_lane = lax.broadcasted_iota(jnp.int32, (WINDOW, BLOCK), 1)
            above = (window_lane > window_row) & (window_lane < end)
            change = contract(
                left_terms(done, 0), right_terms(jnp.where(above, 0.0, done), 0), 0, 0
            )
            rest_lane = lax.broadcasted_iota(jnp.int32, (BLOCK - end, BLOCK), 1)
            taken = (rest_lane >= base) & (rest_lane < end)
            work[end:, :] = jnp.where(taken, 0.0, work[end:, :]) - change[end:, :]


def pack_kernel(prior_ref, bank_ref, half_ref, first_ref):
    row_part, col_part = lax.axis_index("tokens"), lax.axis_index("width")
    on_diagonal = eye_mask()

    def put(rows, columns, value):
        half_ref[rows, columns] = value
        first_ref[rows, columns] = value

    top, left, right = slice(0, BLOCK), slice(0, BLOCK), slice(BLOCK, 2 * BLOCK)

    @pl.when(row_part == col_part)
    def _():
        shape = (BLOCK, BLOCK)
        upper = lax.broadcasted_iota(jnp.int32, shape, 0) <= lax.broadcasted_iota(
            jnp.int32, shape, 1
        )
        put(top, left, jnp.where(upper, prior_ref[:BLOCK, :BLOCK], prior_ref[BLOCK:, BLOCK:]))
        put(top, right, prior_ref[:BLOCK, BLOCK:])

    @pl.when(row_part < col_part)
    def _():
        put(top, slice(None), prior_ref[:BLOCK, :])

    @pl.when(row_part > col_part)
    def _():
        put(top, left, prior_ref[:BLOCK, BLOCK:].T)
        put(top, right, prior_ref[BLOCK:, BLOCK:].T)

    diagonal = jnp.sum(jnp.where(on_diagonal, prior_ref[BLOCK:, BLOCK:], 0.0), axis=0, keepdims=True)
    tail = slice(BLOCK, BLOCK + 8)
    put(tail, left, jnp.broadcast_to(diagonal, (8, BLOCK)))
    put(tail, right, jnp.zeros((8, BLOCK), f32))
    bank_rows = bank_ref.shape[0]
    for c in range(bank_ref.shape[1] // (2 * BLOCK)):
        low = BLOCK + 8 + c * bank_rows
        first_ref[low : low + bank_rows, :] = bank_ref[:, c * 2 * BLOCK : (c + 1) * 2 * BLOCK]


def pack(prior, bank):
    span = BLOCK + 8
    rows = span + bank.size // (2 * BLOCK)
    vmem = pl.BlockSpec(memory_space=pltpu.VMEM)
    return pl.pallas_call(
        pack_kernel,
        out_shape=(
            jax.ShapeDtypeStruct((span, 2 * BLOCK), f32),
            jax.ShapeDtypeStruct((rows, 2 * BLOCK), f32),
        ),
        in_specs=[vmem, vmem],
        out_specs=(vmem, vmem),
    )(prior, bank)


def swap(value, axis, s):
    return lax.ppermute(value, axis, [(i, i ^ s) for i in range(lax.axis_size(axis))])


def exchange(value, axis):
    return [value] + [swap(value, axis, s) for s in range(1, lax.axis_size(axis))]


def solve_kernel(halves, ids_ref, order_ref, *refs):
    if halves:
        own_ref, others_ref, near_ref, far_ref, grads_ref, out_ref = refs[:6]
        gram, extra, work, left_ref, right_ref, tails, bank, sems = refs[6:]
    else:
        prior_ref, bank_ref, grads_ref, out_ref = refs[:4]
        gram, extra, work, left_ref, right_ref, bank, sems = refs[4:]
    size = gram.shape[0]
    blocks = size // BLOCK
    sequences = order_ref.shape[0]
    columns_here, queries = out_ref.shape
    bank_chunks, bank_rows, chunk = bank.shape[1:]
    width_index, token_index = lax.axis_index("width"), lax.axis_index("tokens")
    copies = []

    def start(source, target):
        copy = pltpu.make_async_copy(source, target, sems.at[len(copies)])
        copy.start()
        copies.append(copy)

    if halves:
        parts = own_ref.shape[0]
        span = BLOCK + 8

        def place(source, i, j):
            row = 2 * BLOCK * lax.min(i, j) + jnp.where(i > j, BLOCK, 0)
            row = pl.multiple_of(row, BLOCK)
            column = pl.multiple_of(2 * BLOCK * lax.max(i, j), BLOCK)
            start(
                source.at[:BLOCK, :], gram.at[pl.ds(row, BLOCK), pl.ds(column, 2 * BLOCK)]
            )
            start(source.at[BLOCK:, :], tails.at[i, j])

        for i in range(parts):
            place(own_ref.at[i, :span, :], i, width_index)
            for s in range(2, parts):
                first = (s - 2) * span
                place(
                    others_ref.at[i, first : first + span, :], i, lax.bitwise_xor(width_index, s)
                )
            for c in range(bank_chunks):
                first = span + c * bank_rows
                start(own_ref.at[i, first : first + bank_rows, :], bank.at[i, c])
        for sibling, source in enumerate((near_ref, far_ref)):
            for across in range(2):
                place(
                    source.at[across],
                    lax.bitwise_xor(token_index, 2 * across + sibling),
                    lax.bitwise_xor(width_index, 1),
                )
    else:
        start(prior_ref, gram)
        start(bank_ref, bank)
    slabs = grads_ref.shape[1]
    for i in range(grads_ref.shape[0]):
        extra[i * slabs : (i + 1) * slabs, :] = grads_ref[i]
    grads = extra[:sequences, :]
    left, right = both_terms(grads, 0)
    on_diagonal = eye_mask()
    for copy in copies:
        copy.wait()
    for q in range(queries):
        id_here = ids_ref[token_index * queries + q]
        part, row = id_here // bank_rows, id_here % bank_rows
        for c in range(bank_chunks):
            extra[sequences + q : sequences + q + 1, c * chunk : (c + 1) * chunk] = bank[
                part, c, pl.ds(row, 1), :
            ]
    diagonal = jnp.zeros((BLOCK, BLOCK), f32)
    if halves:
        upper = lax.broadcasted_iota(jnp.int32, (BLOCK, BLOCK), 0) <= lax.broadcasted_iota(
            jnp.int32, (BLOCK, BLOCK), 1
        )
        for i in range(parts):
            low = 2 * BLOCK * i
            mid, high = low + BLOCK, low + 2 * BLOCK
            packed = gram[low:mid, low:mid]
            turned = packed.T
            gram[low:mid, low:mid] = jnp.where(upper, packed, turned)
            second = jnp.where(
                on_diagonal, tails[i, i, 0:1, :BLOCK], jnp.where(upper, turned, packed)
            )
            gram[mid:high, mid:high] = second
            diagonal = diagonal + jnp.where(on_diagonal, packed + second, 0.0)
    else:
        for low in range(0, size, BLOCK):
            diagonal = diagonal + jnp.where(
                on_diagonal, gram[low : low + BLOCK, low : low + BLOCK], 0.0
            )
    trace = jnp.sum(diagonal) + jnp.sum(grads * grads) / sequences
    damping = damping_ratio * trace / size
    for low in range(0, size, BLOCK):
        high = low + BLOCK
        product = contract(left[:, low:high], right[:, low:], 0, 0) / sequences
        gram[low:high, low:high] = (
            gram[low:high, low:high]
            + product[:, :BLOCK]
            + jnp.where(on_diagonal, damping, 0.0)
        )
        if high < size:
            gram[low:high, high:] = gram[low:high, high:] + product[:, BLOCK:]
    scores = [jnp.zeros((queries, sequences), f32)]
    lower = lax.broadcasted_iota(jnp.int32, (BLOCK, BLOCK), 0) >= lax.broadcasted_iota(
        jnp.int32, (BLOCK, BLOCK), 1
    )
    waiting = []

    def pending():
        if waiting:
            waiting.pop(0)()

    def panel(inverse_left, block, low, high):
        left, right = both_terms(
            contract(inverse_left, right_terms(gram[block : block + BLOCK, low:high], 0), 1, 0), 0
        )
        left_ref[:, low:high] = left
        right_ref[:, low:high] = right
        return left, right

    def update(row, low):
        gram[row : row + BLOCK, low:] = gram[row : row + BLOCK, low:] - contract(
            left_ref[:, row : row + BLOCK], right_ref[:, low:], 0, 0
        )

    def update_extra(inverse_right, low, high):
        solved = contract(left_terms(extra[:, low:high], 1), inverse_right, 1, 1)
        solved_left, solved_right = both_terms(solved, 1)
        scores[0] = scores[0] + contract(solved_left[sequences:], solved_right[:sequences], 1, 1)
        if high < size:
            extra[:, high:] = extra[:, high:] - contract(solved_left, right_ref[:, high:], 1, 0)

    for low in range(0, size, BLOCK):
        high = low + BLOCK
        work[...] = gram[low:high, low:high]
        factor_block(work, pending)
        while waiting:
            pending()
        inverse_left, inverse_right = both_terms(jnp.where(lower, work[...], 0.0), 1)
        if high < size:
            after = high + BLOCK
            left, right = panel(inverse_left, low, high, after)
            gram[high:after, high:after] = gram[high:after, high:after] - contract(
                left, right, 0, 0
            )
            if after < size:
                middle = after + ((size - after) // BLOCK + 1) // 2 * BLOCK
                waiting.append(functools.partial(panel, inverse_left, low, after, middle))
                if middle < size:
                    waiting.append(functools.partial(panel, inverse_left, low, middle, size))
                waiting.append(functools.partial(update, high, after))
        waiting.append(functools.partial(update_extra, inverse_right, low, high))
        for row in range(high + BLOCK, size, BLOCK):
            waiting.append(functools.partial(update, row, row))
    while waiting:
        pending()
    shape = (columns_here, sequences)
    column_id = width_index * columns_here + lax.broadcasted_iota(jnp.int32, shape, 0)
    slab_id = lax.broadcasted_iota(jnp.int32, shape, 1)
    choose = jnp.zeros(shape, f32)
    for n in range(sequences):
        choose = jnp.where((slab_id == n) & (column_id == order_ref[n]), 1.0, choose)
    out_ref[...] = lax.dot_general(
        choose, scores[0], (((1,), (1,)), ((), ())), precision=highest
    )


def solve(halves, ids, order, prior_operands, bank_shape, grads, out_shape):
    size = grads.shape[2]
    rows = order.shape[0] + out_shape[1]
    copies = 2 + bank_shape[0] * (2 * bank_shape[0] + bank_shape[1])
    vmem = pl.BlockSpec(memory_space=pltpu.VMEM)
    scratch = [
        pltpu.VMEM((size, size), f32),
        pltpu.VMEM((rows, size), f32),
        pltpu.VMEM((BLOCK, BLOCK), f32),
        pltpu.VMEM((TERMS * BLOCK, size), jnp.bfloat16),
        pltpu.VMEM((TERMS * BLOCK, size), jnp.bfloat16),
    ]
    if halves:
        scratch.append(pltpu.VMEM((bank_shape[0], bank_shape[0], 8, 2 * BLOCK), f32))
    return pl.pallas_call(
        functools.partial(solve_kernel, halves),
        out_shape=jax.ShapeDtypeStruct(out_shape, f32),
        in_specs=[pl.BlockSpec(memory_space=pltpu.SMEM)] * 2
        + [pl.BlockSpec(memory_space=pl.ANY)] * len(prior_operands)
        + [vmem],
        out_specs=vmem,
        scratch_shapes=scratch
        + [pltpu.VMEM(bank_shape, f32), pltpu.SemaphoreType.DMA((copies,))],
        compiler_params=pltpu.CompilerParams(vmem_limit_bytes=60 * 2**20),
        cost_estimate=pl.CostEstimate(
            flops=4 * size**3, bytes_accessed=4 * size * size, transcendentals=size
        ),
    )(ids, order, *prior_operands, grads)


def local(
    layer_inputs,
    output_grads,
    proj_in,
    proj_out,
    prior_gram,
    query_bank,
    slab_sequence,
    seq_lengths,
    query_ids,
):
    width_count = lax.axis_size("width")
    token_count = lax.axis_size("tokens")
    token_index = lax.axis_index("tokens")
    slab_count = layer_inputs.shape[0] // SEQ_LEN
    sequence_count = slab_sequence.shape[0]
    bank_rows = query_bank.shape[0]
    halves = prior_gram.shape == (2 * BLOCK, 2 * BLOCK)

    if halves:
        half, first = pack(prior_gram, query_bank)
        own = lax.all_gather(first, "tokens", axis=0)
        pieces = exchange(half, "width")[1:]
        bank_shape = (token_count, query_bank.shape[1] // (2 * BLOCK), bank_rows, 2 * BLOCK)
    else:
        prior_block = lax.all_gather(prior_gram, "width", axis=1, tiled=True)
        prior_full = lax.all_gather(prior_block, "tokens", axis=0, tiled=True)
        bank_shape = (token_count, 1, bank_rows, query_bank.shape[1])
        bank_full = lax.all_gather(query_bank, "tokens", axis=0, tiled=True)
        prior_operands = (prior_full, bank_full.reshape(bank_shape))

    features = (((1,), (1,)), ((), ()))
    projected = jnp.concatenate(
        [
            lax.dot_general(proj_in, layer_inputs, features, preferred_element_type=f32),
            lax.dot_general(proj_out, output_grads, features, preferred_element_type=f32),
        ],
        axis=0,
    )
    if halves:
        projected, pieces[0] = lax.optimization_barrier((projected, pieces[0]))
    received = exchange(projected, "width")
    if halves:
        received[1], pieces = lax.optimization_barrier((received[1], pieces))
        others = lax.all_gather(jnp.concatenate(pieces[1:], 0), "tokens", axis=0)
        near = jnp.stack([pieces[0], swap(pieces[0], "tokens", 2)])
        prior_operands = (own, others, near, swap(near, "tokens", 1))
    total = sum(received)
    local_slabs = lax.dynamic_slice_in_dim(slab_sequence, token_index * slab_count, slab_count)
    seq_numbers = jnp.arange(sequence_count, dtype=jnp.int32)
    local_lengths = jnp.sum(
        jnp.where(local_slabs[:, None] == seq_numbers[None, :], seq_lengths[None, :], 0), axis=1
    )
    offset = jnp.arange(SEQ_LEN, dtype=jnp.int32)
    valid = (offset[None, :] < local_lengths[:, None]).reshape(1, -1)
    total_in = jnp.where(valid, total[:R_IN], 0.0).reshape(R_IN, slab_count, SEQ_LEN)
    total_out = total[R_IN:].reshape(-1, slab_count, SEQ_LEN)
    vectors = lax.dot_general(
        total_in, total_out, (((2,), (2,)), ((1,), (1,))), precision=highest
    ).reshape(slab_count, K)
    all_grads = lax.all_gather(vectors, "tokens", axis=0)
    out_shape = (sequence_count // width_count, query_ids.shape[0] // token_count)
    return solve(
        halves, query_ids, slab_sequence, prior_operands, bank_shape, all_grads, out_shape
    ).T


def solution(mesh):
    return jax.shard_map(
        local,
        mesh=mesh,
        in_specs=(
            P(("groups", "tokens"), "width"),
            P(("groups", "tokens"), "width"),
            P(None, "width"),
            P(None, "width"),
            P(("groups", "tokens"), "width"),
            P(("groups", "tokens"), None),
            P("groups"),
            P("groups"),
            P("groups"),
        ),
        out_specs=P(("groups", "tokens"), "width"),
        check_vma=False,
    )
```

```python
import functools

import jax
import jax.numpy as jnp
from jax import lax
from jax.experimental import pallas as pl
from jax.experimental.pallas import tpu as pltpu
from jax.sharding import PartitionSpec as P

R_IN = 32
SEQ_LEN = 128
K = 1024
BLOCK = 128
PIVOTS = 16
WINDOW = 32
TERMS = 6
f32 = jnp.float32


damping_ratio = 0.1
highest = lax.Precision.HIGHEST


def split_terms(value):
    high = value.astype(jnp.bfloat16)
    rest = value - high.astype(f32)
    mid = rest.astype(jnp.bfloat16)
    low = (rest - mid.astype(f32)).astype(jnp.bfloat16)
    return high, mid, low


def left_terms(value, axis):
    high, mid, low = split_terms(value)
    return jnp.concatenate([high, high, mid, mid, high, low], axis)


def right_terms(value, axis):
    high, mid, low = split_terms(value)
    return jnp.concatenate([high, mid, high, mid, low, high], axis)


def both_terms(value, axis):
    high, mid, low = split_terms(value)
    return (
        jnp.concatenate([high, high, mid, mid, high, low], axis),
        jnp.concatenate([high, mid, high, mid, low, high], axis),
    )


def contract(a, b, a_dim, b_dim):
    return lax.dot_general(a, b, (((a_dim,), (b_dim,)), ((), ())), preferred_element_type=f32)


def eye_mask():
    shape = (BLOCK, BLOCK)
    return lax.broadcasted_iota(jnp.int32, shape, 0) == lax.broadcasted_iota(jnp.int32, shape, 1)


def factor_block(work, pending):
    row = lax.broadcasted_iota(jnp.int32, (8, BLOCK), 0)
    lane = lax.broadcasted_iota(jnp.int32, (8, BLOCK), 1)
    tiles = WINDOW // 8
    for base in range(0, BLOCK, WINDOW):
        rows = [work[base + 8 * h : base + 8 * h + 8, :] for h in range(tiles)]
        for group in range(0, WINDOW, PIVOTS):
            columns = [
                {
                    h: jnp.broadcast_to(rows[h][:, column : column + 1], (8, BLOCK))
                    for h in range(group // 8, tiles)
                }
                for column in range(base + group, base + group + PIVOTS)
            ]
            pending()
            for j in range(PIVOTS):
                hj, jj = divmod(group + j, 8)
                here = lane == base + group + j
                scale = lax.rsqrt(jnp.broadcast_to(columns[j][hj][jj : jj + 1, :], (8, BLOCK)))
                lower = {h: columns[j][h] * scale for h in range(hj, tiles)}
                for l in range(j + 1, PIVOTS):
                    entry = jnp.broadcast_to(columns[l][hj][jj : jj + 1, :], (8, BLOCK)) * scale
                    for h in range(hj, tiles):
                        columns[l][h] = columns[l][h] - lower[h] * entry
                pivot_row = jnp.broadcast_to(rows[hj][jj : jj + 1, :], (8, BLOCK))
                pivot_row = jnp.where(here, 1.0, pivot_row) * scale
                for h in range(hj, tiles):
                    changed = jnp.where(here, 0.0, rows[h]) - lower[h] * pivot_row
                    if h == hj:
                        changed = jnp.where(
                            row > jj, changed, jnp.where(row == jj, pivot_row, rows[h])
                        )
                    rows[h] = changed
        done = jnp.concatenate(rows, 0)
        end = base + WINDOW
        work[base:end, :] = done
        if end < BLOCK:
            window_row = base + lax.broadcasted_iota(jnp.int32, (WINDOW, BLOCK), 0)
            window_lane = lax.broadcasted_iota(jnp.int32, (WINDOW, BLOCK), 1)
            above = (window_lane > window_row) & (window_lane < end)
            change = contract(
                left_terms(done, 0), right_terms(jnp.where(above, 0.0, done), 0), 0, 0
            )
            rest_lane = lax.broadcasted_iota(jnp.int32, (BLOCK - end, BLOCK), 1)
            taken = (rest_lane >= base) & (rest_lane < end)
            work[end:, :] = jnp.where(taken, 0.0, work[end:, :]) - change[end:, :]


def pack_kernel(prior_ref, bank_ref, half_ref, first_ref):
    row_part, col_part = lax.axis_index("tokens"), lax.axis_index("width")
    on_diagonal = eye_mask()

    def put(rows, columns, value):
        half_ref[rows, columns] = value
        first_ref[rows, columns] = value

    top, left, right = slice(0, BLOCK), slice(0, BLOCK), slice(BLOCK, 2 * BLOCK)

    @pl.when(row_part == col_part)
    def _():
        shape = (BLOCK, BLOCK)
        upper = lax.broadcasted_iota(jnp.int32, shape, 0) <= lax.broadcasted_iota(
            jnp.int32, shape, 1
        )
        put(top, left, jnp.where(upper, prior_ref[:BLOCK, :BLOCK], prior_ref[BLOCK:, BLOCK:]))
        put(top, right, prior_ref[:BLOCK, BLOCK:])

    @pl.when(row_part < col_part)
    def _():
        put(top, slice(None), prior_ref[:BLOCK, :])

    @pl.when(row_part > col_part)
    def _():
        put(top, left, prior_ref[:BLOCK, BLOCK:].T)
        put(top, right, prior_ref[BLOCK:, BLOCK:].T)

    diagonal = jnp.sum(jnp.where(on_diagonal, prior_ref[BLOCK:, BLOCK:], 0.0), axis=0, keepdims=True)
    tail = slice(BLOCK, BLOCK + 8)
    put(tail, left, jnp.broadcast_to(diagonal, (8, BLOCK)))
    put(tail, right, jnp.zeros((8, BLOCK), f32))
    bank_rows = bank_ref.shape[0]
    for c in range(bank_ref.shape[1] // (2 * BLOCK)):
        low = BLOCK + 8 + c * bank_rows
        first_ref[low : low + bank_rows, :] = bank_ref[:, c * 2 * BLOCK : (c + 1) * 2 * BLOCK]


def pack(prior, bank):
    span = BLOCK + 8
    rows = span + bank.size // (2 * BLOCK)
    vmem = pl.BlockSpec(memory_space=pltpu.VMEM)
    return pl.pallas_call(
        pack_kernel,
        out_shape=(
            jax.ShapeDtypeStruct((span, 2 * BLOCK), f32),
            jax.ShapeDtypeStruct((rows, 2 * BLOCK), f32),
        ),
        in_specs=[vmem, vmem],
        out_specs=(vmem, vmem),
    )(prior, bank)


def swap(value, axis, s):
    return lax.ppermute(value, axis, [(i, i ^ s) for i in range(lax.axis_size(axis))])


def solve_kernel(halves, ids_ref, order_ref, *refs):
    if halves:
        own_ref, *piece_refs, grads_ref, out_ref = refs[:7]
        gram, extra, work, left_ref, right_ref, tails, bank, sems = refs[7:]
    else:
        prior_ref, bank_ref, grads_ref, out_ref = refs[:4]
        gram, extra, work, left_ref, right_ref, bank, sems = refs[4:]
    size = gram.shape[0]
    blocks = size // BLOCK
    sequences = order_ref.shape[0]
    columns_here, queries = out_ref.shape
    bank_chunks, bank_rows, chunk = bank.shape[1:]
    width_index, token_index = lax.axis_index("width"), lax.axis_index("tokens")
    copies = []

    def start(source, target):
        copy = pltpu.make_async_copy(source, target, sems.at[len(copies)])
        copy.start()
        copies.append(copy)

    if halves:
        parts = own_ref.shape[0]
        span = BLOCK + 8

        def place(source, i, j):
            row = 2 * BLOCK * lax.min(i, j) + jnp.where(i > j, BLOCK, 0)
            row = pl.multiple_of(row, BLOCK)
            column = pl.multiple_of(2 * BLOCK * lax.max(i, j), BLOCK)
            start(
                source.at[:BLOCK, :], gram.at[pl.ds(row, BLOCK), pl.ds(column, 2 * BLOCK)]
            )
            start(source.at[BLOCK:, :], tails.at[i, j])

        for i in range(parts):
            place(own_ref.at[i, :span, :], i, width_index)
            for c in range(bank_chunks):
                first = span + c * bank_rows
                start(own_ref.at[i, first : first + bank_rows, :], bank.at[i, c])
        for distance, source in enumerate(piece_refs):
            for s in range(1, parts):
                place(
                    source.at[(s - 1) * span : s * span, :],
                    lax.bitwise_xor(token_index, distance),
                    lax.bitwise_xor(width_index, s),
                )
    else:
        start(prior_ref, gram)
        start(bank_ref, bank)
    slabs = grads_ref.shape[1]
    for i in range(grads_ref.shape[0]):
        extra[i * slabs : (i + 1) * slabs, :] = grads_ref[i]
    grads = extra[:sequences, :]
    left, right = both_terms(grads, 0)
    on_diagonal = eye_mask()
    for copy in copies:
        copy.wait()
    for q in range(queries):
        id_here = ids_ref[token_index * queries + q]
        part, row = id_here // bank_rows, id_here % bank_rows
        for c in range(bank_chunks):
            extra[sequences + q : sequences + q + 1, c * chunk : (c + 1) * chunk] = bank[
                part, c, pl.ds(row, 1), :
            ]
    diagonal = jnp.zeros((BLOCK, BLOCK), f32)
    if halves:
        upper = lax.broadcasted_iota(jnp.int32, (BLOCK, BLOCK), 0) <= lax.broadcasted_iota(
            jnp.int32, (BLOCK, BLOCK), 1
        )
        for i in range(parts):
            low = 2 * BLOCK * i
            mid, high = low + BLOCK, low + 2 * BLOCK
            packed = gram[low:mid, low:mid]
            turned = packed.T
            gram[low:mid, low:mid] = jnp.where(upper, packed, turned)
            second = jnp.where(
                on_diagonal, tails[i, i, 0:1, :BLOCK], jnp.where(upper, turned, packed)
            )
            gram[mid:high, mid:high] = second
            diagonal = diagonal + jnp.where(on_diagonal, packed + second, 0.0)
    else:
        for low in range(0, size, BLOCK):
            diagonal = diagonal + jnp.where(
                on_diagonal, gram[low : low + BLOCK, low : low + BLOCK], 0.0
            )
    trace = jnp.sum(diagonal) + jnp.sum(grads * grads) / sequences
    damping = damping_ratio * trace / size
    for low in range(0, size, BLOCK):
        high = low + BLOCK
        product = contract(left[:, low:high], right[:, low:], 0, 0) / sequences
        gram[low:high, low:high] = (
            gram[low:high, low:high]
            + product[:, :BLOCK]
            + jnp.where(on_diagonal, damping, 0.0)
        )
        if high < size:
            gram[low:high, high:] = gram[low:high, high:] + product[:, BLOCK:]
    scores = [jnp.zeros((queries, sequences), f32)]
    lower = lax.broadcasted_iota(jnp.int32, (BLOCK, BLOCK), 0) >= lax.broadcasted_iota(
        jnp.int32, (BLOCK, BLOCK), 1
    )
    waiting = []

    def pending():
        if waiting:
            waiting.pop(0)()

    def panel(inverse_left, block, low, high):
        left, right = both_terms(
            contract(inverse_left, right_terms(gram[block : block + BLOCK, low:high], 0), 1, 0), 0
        )
        left_ref[:, low:high] = left
        right_ref[:, low:high] = right
        return left, right

    def update(row, low):
        gram[row : row + BLOCK, low:] = gram[row : row + BLOCK, low:] - contract(
            left_ref[:, row : row + BLOCK], right_ref[:, low:], 0, 0
        )

    def update_extra(inverse_right, low, high):
        solved = contract(left_terms(extra[:, low:high], 1), inverse_right, 1, 1)
        solved_left, solved_right = both_terms(solved, 1)
        scores[0] = scores[0] + contract(solved_left[sequences:], solved_right[:sequences], 1, 1)
        if high < size:
            extra[:, high:] = extra[:, high:] - contract(solved_left, right_ref[:, high:], 1, 0)

    for low in range(0, size, BLOCK):
        high = low + BLOCK
        work[...] = gram[low:high, low:high]
        factor_block(work, pending)
        while waiting:
            pending()
        inverse_left, inverse_right = both_terms(jnp.where(lower, work[...], 0.0), 1)
        if high < size:
            after = high + BLOCK
            left, right = panel(inverse_left, low, high, after)
            gram[high:after, high:after] = gram[high:after, high:after] - contract(
                left, right, 0, 0
            )
            if after < size:
                middle = after + ((size - after) // BLOCK + 1) // 2 * BLOCK
                waiting.append(functools.partial(panel, inverse_left, low, after, middle))
                if middle < size:
                    waiting.append(functools.partial(panel, inverse_left, low, middle, size))
                waiting.append(functools.partial(update, high, after))
        waiting.append(functools.partial(update_extra, inverse_right, low, high))
        for row in range(high + BLOCK, size, BLOCK):
            waiting.append(functools.partial(update, row, row))
    while waiting:
        pending()
    shape = (columns_here, sequences)
    column_id = width_index * columns_here + lax.broadcasted_iota(jnp.int32, shape, 0)
    slab_id = lax.broadcasted_iota(jnp.int32, shape, 1)
    choose = jnp.zeros(shape, f32)
    for n in range(sequences):
        choose = jnp.where((slab_id == n) & (column_id == order_ref[n]), 1.0, choose)
    out_ref[...] = lax.dot_general(
        choose, scores[0], (((1,), (1,)), ((), ())), precision=highest
    )


def solve(halves, ids, order, prior_operands, bank_shape, grads, out_shape):
    size = grads.shape[2]
    rows = order.shape[0] + out_shape[1]
    copies = 2 + bank_shape[0] * (2 * bank_shape[0] + bank_shape[1])
    near = len(prior_operands) - 1 if halves else 0
    vmem = pl.BlockSpec(memory_space=pltpu.VMEM)
    scratch = [
        pltpu.VMEM((size, size), f32),
        pltpu.VMEM((rows, size), f32),
        pltpu.VMEM((BLOCK, BLOCK), f32),
        pltpu.VMEM((TERMS * BLOCK, size), jnp.bfloat16),
        pltpu.VMEM((TERMS * BLOCK, size), jnp.bfloat16),
    ]
    if halves:
        scratch.append(pltpu.VMEM((bank_shape[0], bank_shape[0], 8, 2 * BLOCK), f32))
    return pl.pallas_call(
        functools.partial(solve_kernel, halves),
        out_shape=jax.ShapeDtypeStruct(out_shape, f32),
        in_specs=[pl.BlockSpec(memory_space=pltpu.SMEM)] * 2
        + [pl.BlockSpec(memory_space=pltpu.HBM)] * (len(prior_operands) - near)
        + [vmem] * near
        + [vmem],
        out_specs=vmem,
        scratch_shapes=scratch
        + [pltpu.VMEM(bank_shape, f32), pltpu.SemaphoreType.DMA((copies,))],
        compiler_params=pltpu.CompilerParams(vmem_limit_bytes=40 * 2**20),
        cost_estimate=pl.CostEstimate(
            flops=4 * size**3, bytes_accessed=4 * size * size, transcendentals=size
        ),
    )(ids, order, *prior_operands, grads)


def local(
    layer_inputs,
    output_grads,
    proj_in,
    proj_out,
    prior_gram,
    query_bank,
    slab_sequence,
    seq_lengths,
    query_ids,
):
    width_count = lax.axis_size("width")
    token_count = lax.axis_size("tokens")
    token_index = lax.axis_index("tokens")
    slab_count = layer_inputs.shape[0] // SEQ_LEN
    sequence_count = slab_sequence.shape[0]
    bank_rows = query_bank.shape[0]
    halves = prior_gram.shape == (2 * BLOCK, 2 * BLOCK)

    if halves:
        half, first = pack(prior_gram, query_bank)
        own = lax.all_gather(first, "tokens", axis=0)
        pieces = [swap(half, "width", s) for s in range(1, width_count)]
        bank_shape = (token_count, query_bank.shape[1] // (2 * BLOCK), bank_rows, 2 * BLOCK)
    else:
        prior_block = lax.all_gather(prior_gram, "width", axis=1, tiled=True)
        prior_full = lax.all_gather(prior_block, "tokens", axis=0, tiled=True)
        bank_shape = (token_count, 1, bank_rows, query_bank.shape[1])
        bank_full = lax.all_gather(query_bank, "tokens", axis=0, tiled=True)
        prior_operands = (prior_full, bank_full.reshape(bank_shape))

    features = (((1,), (1,)), ((), ()))
    projected = jnp.concatenate(
        [
            lax.dot_general(proj_in, layer_inputs, features, preferred_element_type=f32),
            lax.dot_general(proj_out, output_grads, features, preferred_element_type=f32),
        ],
        axis=0,
    )
    if halves:
        projected, pieces[0] = lax.optimization_barrier((projected, pieces[0]))
    total = projected + swap(projected, "width", 1)
    if halves:
        total, pieces = lax.optimization_barrier((total, pieces))
        pieces = jnp.concatenate(pieces, 0)
        across = swap(pieces, "tokens", 2)
        prior_operands = (
            own,
            pieces,
            swap(pieces, "tokens", 1),
            across,
            swap(across, "tokens", 1),
        )
    distance = 2
    while distance < width_count:
        total = total + swap(total, "width", distance)
        distance *= 2
    local_slabs = lax.dynamic_slice_in_dim(slab_sequence, token_index * slab_count, slab_count)
    seq_numbers = jnp.arange(sequence_count, dtype=jnp.int32)
    local_lengths = jnp.sum(
        jnp.where(local_slabs[:, None] == seq_numbers[None, :], seq_lengths[None, :], 0), axis=1
    )
    offset = jnp.arange(SEQ_LEN, dtype=jnp.int32)
    valid = (offset[None, :] < local_lengths[:, None]).reshape(1, -1)
    total_in = jnp.where(valid, total[:R_IN], 0.0).reshape(R_IN, slab_count, SEQ_LEN)
    total_out = total[R_IN:].reshape(-1, slab_count, SEQ_LEN)
    vectors = lax.dot_general(
        total_in, total_out, (((2,), (2,)), ((1,), (1,))), precision=highest
    ).reshape(slab_count, K)
    all_grads = lax.all_gather(vectors, "tokens", axis=0)
    out_shape = (sequence_count // width_count, query_ids.shape[0] // token_count)
    return solve(
        halves, query_ids, slab_sequence, prior_operands, bank_shape, all_grads, out_shape
    ).T


def solution(mesh):
    return jax.shard_map(
        local,
        mesh=mesh,
        in_specs=(
            P(("groups", "tokens"), "width"),
            P(("groups", "tokens"), "width"),
            P(None, "width"),
            P(None, "width"),
            P(("groups", "tokens"), "width"),
            P(("groups", "tokens"), None),
            P("groups"),
            P("groups"),
            P("groups"),
        ),
        out_specs=P(("groups", "tokens"), "width"),
        check_vma=False,
    )
```

```python
import functools

import jax
import jax.numpy as jnp
from jax import lax
from jax.experimental import pallas as pl
from jax.experimental.pallas import tpu as pltpu
from jax.sharding import PartitionSpec as P

R_IN = 32
SEQ_LEN = 128
K = 1024
BLOCK = 128
PIVOTS = 16
WINDOW = 32
TERMS = 6
f32 = jnp.float32


damping_ratio = 0.1
highest = lax.Precision.HIGHEST


def split_terms(value):
    high = value.astype(jnp.bfloat16)
    rest = value - high.astype(f32)
    mid = rest.astype(jnp.bfloat16)
    low = (rest - mid.astype(f32)).astype(jnp.bfloat16)
    return high, mid, low


def left_terms(value, axis):
    high, mid, low = split_terms(value)
    return jnp.concatenate([high, high, mid, mid, high, low], axis)


def right_terms(value, axis):
    high, mid, low = split_terms(value)
    return jnp.concatenate([high, mid, high, mid, low, high], axis)


def both_terms(value, axis):
    high, mid, low = split_terms(value)
    return (
        jnp.concatenate([high, high, mid, mid, high, low], axis),
        jnp.concatenate([high, mid, high, mid, low, high], axis),
    )


def contract(a, b, a_dim, b_dim):
    return lax.dot_general(a, b, (((a_dim,), (b_dim,)), ((), ())), preferred_element_type=f32)


def eye_mask():
    shape = (BLOCK, BLOCK)
    return lax.broadcasted_iota(jnp.int32, shape, 0) == lax.broadcasted_iota(jnp.int32, shape, 1)


def factor_block(work, pending):
    row = lax.broadcasted_iota(jnp.int32, (8, BLOCK), 0)
    lane = lax.broadcasted_iota(jnp.int32, (8, BLOCK), 1)
    tiles = WINDOW // 8
    for base in range(0, BLOCK, WINDOW):
        rows = [work[base + 8 * h : base + 8 * h + 8, :] for h in range(tiles)]
        for group in range(0, WINDOW, PIVOTS):
            columns = [
                {
                    h: jnp.broadcast_to(rows[h][:, column : column + 1], (8, BLOCK))
                    for h in range(group // 8, tiles)
                }
                for column in range(base + group, base + group + PIVOTS)
            ]
            pending()
            for j in range(PIVOTS):
                hj, jj = divmod(group + j, 8)
                here = lane == base + group + j
                scale = lax.rsqrt(jnp.broadcast_to(columns[j][hj][jj : jj + 1, :], (8, BLOCK)))
                lower = {h: columns[j][h] * scale for h in range(hj, tiles)}
                for l in range(j + 1, PIVOTS):
                    entry = jnp.broadcast_to(columns[l][hj][jj : jj + 1, :], (8, BLOCK)) * scale
                    for h in range(hj, tiles):
                        columns[l][h] = columns[l][h] - lower[h] * entry
                pivot_row = jnp.broadcast_to(rows[hj][jj : jj + 1, :], (8, BLOCK))
                pivot_row = jnp.where(here, 1.0, pivot_row) * scale
                for h in range(hj, tiles):
                    changed = jnp.where(here, 0.0, rows[h]) - lower[h] * pivot_row
                    if h == hj:
                        changed = jnp.where(
                            row > jj, changed, jnp.where(row == jj, pivot_row, rows[h])
                        )
                    rows[h] = changed
        done = jnp.concatenate(rows, 0)
        end = base + WINDOW
        work[base:end, :] = done
        if end < BLOCK:
            window_row = base + lax.broadcasted_iota(jnp.int32, (WINDOW, BLOCK), 0)
            window_lane = lax.broadcasted_iota(jnp.int32, (WINDOW, BLOCK), 1)
            above = (window_lane > window_row) & (window_lane < end)
            change = contract(
                left_terms(done, 0), right_terms(jnp.where(above, 0.0, done), 0), 0, 0
            )
            rest_lane = lax.broadcasted_iota(jnp.int32, (BLOCK - end, BLOCK), 1)
            taken = (rest_lane >= base) & (rest_lane < end)
            work[end:, :] = jnp.where(taken, 0.0, work[end:, :]) - change[end:, :]


def pack_kernel(prior_ref, bank_ref, half_ref, first_ref):
    row_part, col_part = lax.axis_index("tokens"), lax.axis_index("width")
    on_diagonal = eye_mask()

    def put(rows, columns, value):
        half_ref[rows, columns] = value
        first_ref[rows, columns] = value

    top, left, right = slice(0, BLOCK), slice(0, BLOCK), slice(BLOCK, 2 * BLOCK)

    @pl.when(row_part == col_part)
    def _():
        shape = (BLOCK, BLOCK)
        upper = lax.broadcasted_iota(jnp.int32, shape, 0) <= lax.broadcasted_iota(
            jnp.int32, shape, 1
        )
        put(top, left, jnp.where(upper, prior_ref[:BLOCK, :BLOCK], prior_ref[BLOCK:, BLOCK:]))
        put(top, right, prior_ref[:BLOCK, BLOCK:])

    @pl.when(row_part < col_part)
    def _():
        put(top, slice(None), prior_ref[:BLOCK, :])

    @pl.when(row_part > col_part)
    def _():
        put(top, left, prior_ref[:BLOCK, BLOCK:].T)
        put(top, right, prior_ref[BLOCK:, BLOCK:].T)

    diagonal = jnp.sum(jnp.where(on_diagonal, prior_ref[BLOCK:, BLOCK:], 0.0), axis=0, keepdims=True)
    tail = slice(BLOCK, BLOCK + 8)
    put(tail, left, jnp.broadcast_to(diagonal, (8, BLOCK)))
    put(tail, right, jnp.zeros((8, BLOCK), f32))
    bank_rows = bank_ref.shape[0]
    for c in range(bank_ref.shape[1] // (2 * BLOCK)):
        low = BLOCK + 8 + c * bank_rows
        first_ref[low : low + bank_rows, :] = bank_ref[:, c * 2 * BLOCK : (c + 1) * 2 * BLOCK]


def pack(prior, bank):
    span = BLOCK + 8
    rows = span + bank.size // (2 * BLOCK)
    vmem = pl.BlockSpec(memory_space=pltpu.VMEM)
    return pl.pallas_call(
        pack_kernel,
        out_shape=(
            jax.ShapeDtypeStruct((span, 2 * BLOCK), f32),
            jax.ShapeDtypeStruct((rows, 2 * BLOCK), f32),
        ),
        in_specs=[vmem, vmem],
        out_specs=(vmem, vmem),
    )(prior, bank)


def swap(value, axis, s):
    return lax.ppermute(value, axis, [(i, i ^ s) for i in range(lax.axis_size(axis))])


def solve_kernel(halves, ids_ref, order_ref, *refs):
    if halves:
        own_ref, *piece_refs, grads_ref, out_ref = refs[:7]
        gram, extra, work, left_ref, right_ref, tails, bank, sems = refs[7:]
    else:
        prior_ref, bank_ref, grads_ref, out_ref = refs[:4]
        gram, extra, work, left_ref, right_ref, bank, sems = refs[4:]
    size = gram.shape[0]
    blocks = size // BLOCK
    sequences = order_ref.shape[0]
    columns_here, queries = out_ref.shape
    bank_chunks, bank_rows, chunk = bank.shape[1:]
    width_index, token_index = lax.axis_index("width"), lax.axis_index("tokens")
    copies = []

    def start(source, target):
        copy = pltpu.make_async_copy(source, target, sems.at[len(copies)])
        copy.start()
        copies.append(copy)

    if halves:
        parts = own_ref.shape[0]
        span = BLOCK + 8

        def place(source, i, j):
            row = 2 * BLOCK * lax.min(i, j) + jnp.where(i > j, BLOCK, 0)
            row = pl.multiple_of(row, BLOCK)
            column = pl.multiple_of(2 * BLOCK * lax.max(i, j), BLOCK)
            start(
                source.at[:BLOCK, :], gram.at[pl.ds(row, BLOCK), pl.ds(column, 2 * BLOCK)]
            )
            start(source.at[BLOCK:, :], tails.at[i, j])

        for i in range(parts):
            place(own_ref.at[i, :span, :], i, width_index)
            for c in range(bank_chunks):
                first = span + c * bank_rows
                start(own_ref.at[i, first : first + bank_rows, :], bank.at[i, c])
        for distance, source in enumerate(piece_refs):
            for s in range(1, parts):
                place(
                    source.at[(s - 1) * span : s * span, :],
                    lax.bitwise_xor(token_index, distance),
                    lax.bitwise_xor(width_index, s),
                )
    else:
        start(prior_ref, gram)
        start(bank_ref, bank)
    slabs = grads_ref.shape[1]
    for i in range(grads_ref.shape[0]):
        extra[i * slabs : (i + 1) * slabs, :] = grads_ref[i]
    grads = extra[:sequences, :]
    left, right = both_terms(grads, 0)
    on_diagonal = eye_mask()
    for copy in copies:
        copy.wait()
    for q in range(queries):
        id_here = ids_ref[token_index * queries + q]
        part, row = id_here // bank_rows, id_here % bank_rows
        for c in range(bank_chunks):
            extra[sequences + q : sequences + q + 1, c * chunk : (c + 1) * chunk] = bank[
                part, c, pl.ds(row, 1), :
            ]
    diagonal = jnp.zeros((BLOCK, BLOCK), f32)
    if halves:
        upper = lax.broadcasted_iota(jnp.int32, (BLOCK, BLOCK), 0) <= lax.broadcasted_iota(
            jnp.int32, (BLOCK, BLOCK), 1
        )
        for i in range(parts):
            low = 2 * BLOCK * i
            mid, high = low + BLOCK, low + 2 * BLOCK
            packed = gram[low:mid, low:mid]
            turned = packed.T
            gram[low:mid, low:mid] = jnp.where(upper, packed, turned)
            second = jnp.where(
                on_diagonal, tails[i, i, 0:1, :BLOCK], jnp.where(upper, turned, packed)
            )
            gram[mid:high, mid:high] = second
            diagonal = diagonal + jnp.where(on_diagonal, packed + second, 0.0)
    else:
        for low in range(0, size, BLOCK):
            diagonal = diagonal + jnp.where(
                on_diagonal, gram[low : low + BLOCK, low : low + BLOCK], 0.0
            )
    trace = jnp.sum(diagonal) + jnp.sum(grads * grads) / sequences
    damping = damping_ratio * trace / size
    waiting = []

    def pending():
        if waiting:
            waiting.pop(0)()

    def add_product(low):
        high = low + BLOCK
        product = contract(left[:, low:high], right[:, low:], 0, 0) / sequences
        gram[low:high, low:high] = (
            gram[low:high, low:high]
            + product[:, :BLOCK]
            + jnp.where(on_diagonal, damping, 0.0)
        )
        if high < size:
            gram[low:high, high:] = gram[low:high, high:] + product[:, BLOCK:]

    add_product(0)
    for low in range(BLOCK, size, BLOCK):
        waiting.append(functools.partial(add_product, low))
    scores = [jnp.zeros((queries, sequences), f32)]
    lower = lax.broadcasted_iota(jnp.int32, (BLOCK, BLOCK), 0) >= lax.broadcasted_iota(
        jnp.int32, (BLOCK, BLOCK), 1
    )
    def panel(inverse_left, block, low, high):
        left, right = both_terms(
            contract(inverse_left, right_terms(gram[block : block + BLOCK, low:high], 0), 1, 0), 0
        )
        left_ref[:, low:high] = left
        right_ref[:, low:high] = right
        return left, right

    def update(row, low):
        gram[row : row + BLOCK, low:] = gram[row : row + BLOCK, low:] - contract(
            left_ref[:, row : row + BLOCK], right_ref[:, low:], 0, 0
        )

    def update_extra(inverse_right, low, high):
        solved = contract(left_terms(extra[:, low:high], 1), inverse_right, 1, 1)
        solved_left, solved_right = both_terms(solved, 1)
        scores[0] = scores[0] + contract(solved_left[sequences:], solved_right[:sequences], 1, 1)
        if high < size:
            extra[:, high:] = extra[:, high:] - contract(solved_left, right_ref[:, high:], 1, 0)

    for low in range(0, size, BLOCK):
        high = low + BLOCK
        work[...] = gram[low:high, low:high]
        factor_block(work, pending)
        while waiting:
            pending()
        inverse_left, inverse_right = both_terms(jnp.where(lower, work[...], 0.0), 1)
        if high < size:
            after = high + BLOCK
            left, right = panel(inverse_left, low, high, after)
            gram[high:after, high:after] = gram[high:after, high:after] - contract(
                left, right, 0, 0
            )
            if after < size:
                middle = after + ((size - after) // BLOCK + 1) // 2 * BLOCK
                waiting.append(functools.partial(panel, inverse_left, low, after, middle))
                if middle < size:
                    waiting.append(functools.partial(panel, inverse_left, low, middle, size))
                waiting.append(functools.partial(update, high, after))
        waiting.append(functools.partial(update_extra, inverse_right, low, high))
        for row in range(high + BLOCK, size, BLOCK):
            waiting.append(functools.partial(update, row, row))
    while waiting:
        pending()
    shape = (columns_here, sequences)
    column_id = width_index * columns_here + lax.broadcasted_iota(jnp.int32, shape, 0)
    slab_id = lax.broadcasted_iota(jnp.int32, shape, 1)
    choose = jnp.zeros(shape, f32)
    for n in range(sequences):
        choose = jnp.where((slab_id == n) & (column_id == order_ref[n]), 1.0, choose)
    out_ref[...] = lax.dot_general(
        choose, scores[0], (((1,), (1,)), ((), ())), precision=highest
    )


def solve(halves, ids, order, prior_operands, bank_shape, grads, out_shape):
    size = grads.shape[2]
    rows = order.shape[0] + out_shape[1]
    copies = 2 + bank_shape[0] * (2 * bank_shape[0] + bank_shape[1])
    near = len(prior_operands) - 1 if halves else 0
    vmem = pl.BlockSpec(memory_space=pltpu.VMEM)
    scratch = [
        pltpu.VMEM((size, size), f32),
        pltpu.VMEM((rows, size), f32),
        pltpu.VMEM((BLOCK, BLOCK), f32),
        pltpu.VMEM((TERMS * BLOCK, size), jnp.bfloat16),
        pltpu.VMEM((TERMS * BLOCK, size), jnp.bfloat16),
    ]
    if halves:
        scratch.append(pltpu.VMEM((bank_shape[0], bank_shape[0], 8, 2 * BLOCK), f32))
    return pl.pallas_call(
        functools.partial(solve_kernel, halves),
        out_shape=jax.ShapeDtypeStruct(out_shape, f32),
        in_specs=[pl.BlockSpec(memory_space=pltpu.SMEM)] * 2
        + [pl.BlockSpec(memory_space=pltpu.HBM)] * (len(prior_operands) - near)
        + [vmem] * near
        + [vmem],
        out_specs=vmem,
        scratch_shapes=scratch
        + [pltpu.VMEM(bank_shape, f32), pltpu.SemaphoreType.DMA((copies,))],
        compiler_params=pltpu.CompilerParams(vmem_limit_bytes=52 * 2**20),
        cost_estimate=pl.CostEstimate(
            flops=4 * size**3, bytes_accessed=4 * size * size, transcendentals=size
        ),
    )(ids, order, *prior_operands, grads)


def local(
    layer_inputs,
    output_grads,
    proj_in,
    proj_out,
    prior_gram,
    query_bank,
    slab_sequence,
    seq_lengths,
    query_ids,
):
    width_count = lax.axis_size("width")
    token_count = lax.axis_size("tokens")
    token_index = lax.axis_index("tokens")
    slab_count = layer_inputs.shape[0] // SEQ_LEN
    sequence_count = slab_sequence.shape[0]
    bank_rows = query_bank.shape[0]
    halves = prior_gram.shape == (2 * BLOCK, 2 * BLOCK)

    if halves:
        half, first = pack(prior_gram, query_bank)
        own = lax.all_gather(first, "tokens", axis=0)
        pieces = [swap(half, "width", s) for s in range(1, width_count)]
        bank_shape = (token_count, query_bank.shape[1] // (2 * BLOCK), bank_rows, 2 * BLOCK)
    else:
        prior_block = lax.all_gather(prior_gram, "width", axis=1, tiled=True)
        prior_full = lax.all_gather(prior_block, "tokens", axis=0, tiled=True)
        bank_shape = (token_count, 1, bank_rows, query_bank.shape[1])
        bank_full = lax.all_gather(query_bank, "tokens", axis=0, tiled=True)
        prior_operands = (prior_full, bank_full.reshape(bank_shape))

    features = (((1,), (1,)), ((), ()))
    projected = jnp.concatenate(
        [
            lax.dot_general(proj_in, layer_inputs, features, preferred_element_type=f32),
            lax.dot_general(proj_out, output_grads, features, preferred_element_type=f32),
        ],
        axis=0,
    )
    if halves:
        projected, pieces[0] = lax.optimization_barrier((projected, pieces[0]))
    total = projected + swap(projected, "width", 1)
    if halves:
        total, pieces = lax.optimization_barrier((total, pieces))
        pieces = jnp.concatenate(pieces, 0)
        across = swap(pieces, "tokens", 2)
        prior_operands = (
            own,
            pieces,
            swap(pieces, "tokens", 1),
            across,
            swap(across, "tokens", 1),
        )
    distance = 2
    while distance < width_count:
        total = total + swap(total, "width", distance)
        distance *= 2
    local_slabs = lax.dynamic_slice_in_dim(slab_sequence, token_index * slab_count, slab_count)
    seq_numbers = jnp.arange(sequence_count, dtype=jnp.int32)
    local_lengths = jnp.sum(
        jnp.where(local_slabs[:, None] == seq_numbers[None, :], seq_lengths[None, :], 0), axis=1
    )
    offset = jnp.arange(SEQ_LEN, dtype=jnp.int32)
    valid = (offset[None, :] < local_lengths[:, None]).reshape(1, -1)
    total_in = jnp.where(valid, total[:R_IN], 0.0).reshape(R_IN, slab_count, SEQ_LEN)
    total_out = total[R_IN:].reshape(-1, slab_count, SEQ_LEN)
    vectors = lax.dot_general(
        total_in, total_out, (((2,), (2,)), ((1,), (1,))), precision=highest
    ).reshape(slab_count, K)
    all_grads = lax.all_gather(vectors, "tokens", axis=0)
    out_shape = (sequence_count // width_count, query_ids.shape[0] // token_count)
    return solve(
        halves, query_ids, slab_sequence, prior_operands, bank_shape, all_grads, out_shape
    ).T


def solution(mesh):
    return jax.shard_map(
        local,
        mesh=mesh,
        in_specs=(
            P(("groups", "tokens"), "width"),
            P(("groups", "tokens"), "width"),
            P(None, "width"),
            P(None, "width"),
            P(("groups", "tokens"), "width"),
            P(("groups", "tokens"), None),
            P("groups"),
            P("groups"),
            P("groups"),
        ),
        out_specs=P(("groups", "tokens"), "width"),
        check_vma=False,
    )
```

```python
import functools

import jax
import jax.numpy as jnp
from jax import lax
from jax.experimental import pallas as pl
from jax.experimental.pallas import tpu as pltpu
from jax.sharding import PartitionSpec as P

R_IN = 32
SEQ_LEN = 128
K = 1024
BLOCK = 128
PIVOTS = 16
WINDOW = 32
TERMS = 6
f32 = jnp.float32


damping_ratio = 0.1
highest = lax.Precision.HIGHEST


def split_terms(value):
    high = value.astype(jnp.bfloat16)
    rest = value - high.astype(f32)
    mid = rest.astype(jnp.bfloat16)
    low = (rest - mid.astype(f32)).astype(jnp.bfloat16)
    return high, mid, low


def left_terms(value, axis):
    high, mid, low = split_terms(value)
    return jnp.concatenate([high, high, mid, mid, high, low], axis)


def right_terms(value, axis):
    high, mid, low = split_terms(value)
    return jnp.concatenate([high, mid, high, mid, low, high], axis)


def both_terms(value, axis):
    high, mid, low = split_terms(value)
    return (
        jnp.concatenate([high, high, mid, mid, high, low], axis),
        jnp.concatenate([high, mid, high, mid, low, high], axis),
    )


def contract(a, b, a_dim, b_dim):
    return lax.dot_general(a, b, (((a_dim,), (b_dim,)), ((), ())), preferred_element_type=f32)


def eye_mask():
    shape = (BLOCK, BLOCK)
    return lax.broadcasted_iota(jnp.int32, shape, 0) == lax.broadcasted_iota(jnp.int32, shape, 1)


def factor_block(work, pending):
    row = lax.broadcasted_iota(jnp.int32, (8, BLOCK), 0)
    lane = lax.broadcasted_iota(jnp.int32, (8, BLOCK), 1)
    tiles = WINDOW // 8
    for base in range(0, BLOCK, WINDOW):
        rows = [work[base + 8 * h : base + 8 * h + 8, :] for h in range(tiles)]
        for group in range(0, WINDOW, PIVOTS):
            columns = [
                {
                    h: jnp.broadcast_to(rows[h][:, column : column + 1], (8, BLOCK))
                    for h in range(group // 8, tiles)
                }
                for column in range(base + group, base + group + PIVOTS)
            ]
            pending()
            for j in range(PIVOTS):
                hj, jj = divmod(group + j, 8)
                here = lane == base + group + j
                scale = lax.rsqrt(jnp.broadcast_to(columns[j][hj][jj : jj + 1, :], (8, BLOCK)))
                lower = {h: columns[j][h] * scale for h in range(hj, tiles)}
                for l in range(j + 1, PIVOTS):
                    entry = jnp.broadcast_to(columns[l][hj][jj : jj + 1, :], (8, BLOCK)) * scale
                    for h in range(hj, tiles):
                        columns[l][h] = columns[l][h] - lower[h] * entry
                pivot_row = jnp.broadcast_to(rows[hj][jj : jj + 1, :], (8, BLOCK))
                pivot_row = jnp.where(here, 1.0, pivot_row) * scale
                for h in range(hj, tiles):
                    changed = jnp.where(here, 0.0, rows[h]) - lower[h] * pivot_row
                    if h == hj:
                        changed = jnp.where(
                            row > jj, changed, jnp.where(row == jj, pivot_row, rows[h])
                        )
                    rows[h] = changed
        done = jnp.concatenate(rows, 0)
        end = base + WINDOW
        work[base:end, :] = done
        if end < BLOCK:
            window_row = base + lax.broadcasted_iota(jnp.int32, (WINDOW, BLOCK), 0)
            window_lane = lax.broadcasted_iota(jnp.int32, (WINDOW, BLOCK), 1)
            above = (window_lane > window_row) & (window_lane < end)
            change = contract(
                left_terms(done, 0), right_terms(jnp.where(above, 0.0, done), 0), 0, 0
            )
            rest_lane = lax.broadcasted_iota(jnp.int32, (BLOCK - end, BLOCK), 1)
            taken = (rest_lane >= base) & (rest_lane < end)
            work[end:, :] = jnp.where(taken, 0.0, work[end:, :]) - change[end:, :]


def pack_kernel(prior_ref, bank_ref, half_ref, first_ref):
    row_part, col_part = lax.axis_index("tokens"), lax.axis_index("width")
    on_diagonal = eye_mask()

    def put(rows, columns, value):
        half_ref[rows, columns] = value
        first_ref[rows, columns] = value

    top, left, right = slice(0, BLOCK), slice(0, BLOCK), slice(BLOCK, 2 * BLOCK)

    @pl.when(row_part == col_part)
    def _():
        shape = (BLOCK, BLOCK)
        upper = lax.broadcasted_iota(jnp.int32, shape, 0) <= lax.broadcasted_iota(
            jnp.int32, shape, 1
        )
        put(top, left, jnp.where(upper, prior_ref[:BLOCK, :BLOCK], prior_ref[BLOCK:, BLOCK:]))
        put(top, right, prior_ref[:BLOCK, BLOCK:])

    @pl.when(row_part < col_part)
    def _():
        put(top, slice(None), prior_ref[:BLOCK, :])

    @pl.when(row_part > col_part)
    def _():
        put(top, left, prior_ref[:BLOCK, BLOCK:].T)
        put(top, right, prior_ref[BLOCK:, BLOCK:].T)

    diagonal = jnp.sum(jnp.where(on_diagonal, prior_ref[BLOCK:, BLOCK:], 0.0), axis=0, keepdims=True)
    tail = slice(BLOCK, BLOCK + 8)
    put(tail, left, jnp.broadcast_to(diagonal, (8, BLOCK)))
    put(tail, right, jnp.zeros((8, BLOCK), f32))
    bank_rows = bank_ref.shape[0]
    for c in range(bank_ref.shape[1] // (2 * BLOCK)):
        low = BLOCK + 8 + c * bank_rows
        first_ref[low : low + bank_rows, :] = bank_ref[:, c * 2 * BLOCK : (c + 1) * 2 * BLOCK]


def pack(prior, bank):
    span = BLOCK + 8
    rows = span + bank.size // (2 * BLOCK)
    vmem = pl.BlockSpec(memory_space=pltpu.VMEM)
    return pl.pallas_call(
        pack_kernel,
        out_shape=(
            jax.ShapeDtypeStruct((span, 2 * BLOCK), f32),
            jax.ShapeDtypeStruct((rows, 2 * BLOCK), f32),
        ),
        in_specs=[vmem, vmem],
        out_specs=(vmem, vmem),
    )(prior, bank)


def swap(value, axis, s):
    return lax.ppermute(value, axis, [(i, i ^ s) for i in range(lax.axis_size(axis))])


def solve_kernel(halves, ids_ref, order_ref, *refs):
    if halves:
        own_ref, *piece_refs, grads_ref, out_ref = refs[:7]
        gram, extra, work, left_ref, right_ref, tails, bank, sems = refs[7:]
    else:
        prior_ref, bank_ref, grads_ref, out_ref = refs[:4]
        gram, extra, work, left_ref, right_ref, bank, sems = refs[4:]
    size = gram.shape[0]
    blocks = size // BLOCK
    sequences = order_ref.shape[0]
    columns_here, queries = out_ref.shape
    bank_chunks, bank_rows, chunk = bank.shape[1:]
    width_index, token_index = lax.axis_index("width"), lax.axis_index("tokens")
    copies = []

    def start(source, target):
        copy = pltpu.make_async_copy(source, target, sems.at[len(copies)])
        copy.start()
        copies.append(copy)

    if halves:
        parts = own_ref.shape[0]
        span = BLOCK + 8

        def place(source, i, j):
            row = 2 * BLOCK * lax.min(i, j) + jnp.where(i > j, BLOCK, 0)
            row = pl.multiple_of(row, BLOCK)
            column = pl.multiple_of(2 * BLOCK * lax.max(i, j), BLOCK)
            start(
                source.at[:BLOCK, :], gram.at[pl.ds(row, BLOCK), pl.ds(column, 2 * BLOCK)]
            )
            start(source.at[BLOCK:, :], tails.at[i, j])

        for i in range(parts):
            place(own_ref.at[i, :span, :], i, width_index)
            for c in range(bank_chunks):
                first = span + c * bank_rows
                start(own_ref.at[i, first : first + bank_rows, :], bank.at[i, c])
        for distance, source in enumerate(piece_refs):
            for s in range(1, parts):
                place(
                    source.at[(s - 1) * span : s * span, :],
                    lax.bitwise_xor(token_index, distance),
                    lax.bitwise_xor(width_index, s),
                )
    else:
        start(prior_ref, gram)
        start(bank_ref, bank)
    slabs = grads_ref.shape[1]
    for i in range(grads_ref.shape[0]):
        extra[i * slabs : (i + 1) * slabs, :] = grads_ref[i]
    grads = extra[:sequences, :]
    left, right = both_terms(grads, 0)
    on_diagonal = eye_mask()
    for copy in copies:
        copy.wait()
    for q in range(queries):
        id_here = ids_ref[token_index * queries + q]
        part, row = id_here // bank_rows, id_here % bank_rows
        for c in range(bank_chunks):
            extra[sequences + q : sequences + q + 1, c * chunk : (c + 1) * chunk] = bank[
                part, c, pl.ds(row, 1), :
            ]
    diagonal = jnp.zeros((BLOCK, BLOCK), f32)
    if halves:
        upper = lax.broadcasted_iota(jnp.int32, (BLOCK, BLOCK), 0) <= lax.broadcasted_iota(
            jnp.int32, (BLOCK, BLOCK), 1
        )
        for i in range(parts):
            low = 2 * BLOCK * i
            mid, high = low + BLOCK, low + 2 * BLOCK
            packed = gram[low:mid, low:mid]
            turned = packed.T
            gram[low:mid, low:mid] = jnp.where(upper, packed, turned)
            second = jnp.where(
                on_diagonal, tails[i, i, 0:1, :BLOCK], jnp.where(upper, turned, packed)
            )
            gram[mid:high, mid:high] = second
            diagonal = diagonal + jnp.where(on_diagonal, packed + second, 0.0)
    else:
        for low in range(0, size, BLOCK):
            diagonal = diagonal + jnp.where(
                on_diagonal, gram[low : low + BLOCK, low : low + BLOCK], 0.0
            )
    trace = jnp.sum(diagonal) + jnp.sum(grads * grads) / sequences
    damping = damping_ratio * trace / size
    waiting = []

    def pending():
        if waiting:
            waiting.pop(0)()

    def add_product(low):
        high = low + BLOCK
        product = contract(left[:, low:high], right[:, low:], 0, 0) / sequences
        gram[low:high, low:high] = (
            gram[low:high, low:high]
            + product[:, :BLOCK]
            + jnp.where(on_diagonal, damping, 0.0)
        )
        if high < size:
            gram[low:high, high:] = gram[low:high, high:] + product[:, BLOCK:]

    add_product(0)
    for low in range(BLOCK, size, BLOCK):
        waiting.append(functools.partial(add_product, low))
    scores = [jnp.zeros((queries, sequences), f32)]
    lower = lax.broadcasted_iota(jnp.int32, (BLOCK, BLOCK), 0) >= lax.broadcasted_iota(
        jnp.int32, (BLOCK, BLOCK), 1
    )
    def panel(inverse_left, block, low, high):
        left, right = both_terms(
            contract(inverse_left, right_terms(gram[block : block + BLOCK, low:high], 0), 1, 0), 0
        )
        left_ref[:, low:high] = left
        right_ref[:, low:high] = right
        return left, right

    def update(row, low):
        gram[row : row + BLOCK, low:] = gram[row : row + BLOCK, low:] - contract(
            left_ref[:, row : row + BLOCK], right_ref[:, low:], 0, 0
        )

    def update_extra(inverse_right, low, high):
        solved = contract(left_terms(extra[:, low:high], 1), inverse_right, 1, 1)
        solved_left, solved_right = both_terms(solved, 1)
        scores[0] = scores[0] + contract(solved_left[sequences:], solved_right[:sequences], 1, 1)
        if high < size:
            extra[:, high:] = extra[:, high:] - contract(solved_left, right_ref[:, high:], 1, 0)

    for low in range(0, size, BLOCK):
        high = low + BLOCK
        work[...] = gram[low:high, low:high]
        factor_block(work, pending)
        while waiting:
            pending()
        inverse_left, inverse_right = both_terms(jnp.where(lower, work[...], 0.0), 1)
        if high < size:
            after = high + BLOCK
            left, right = panel(inverse_left, low, high, after)
            gram[high:after, high:after] = gram[high:after, high:after] - contract(
                left, right, 0, 0
            )
            if after < size:
                middle = after + ((size - after) // BLOCK + 1) // 2 * BLOCK
                waiting.append(functools.partial(panel, inverse_left, low, after, middle))
                if middle < size:
                    waiting.append(functools.partial(panel, inverse_left, low, middle, size))
                waiting.append(functools.partial(update, high, after))
        waiting.append(functools.partial(update_extra, inverse_right, low, high))
        for row in range(high + BLOCK, size, BLOCK):
            waiting.append(functools.partial(update, row, row))
    while waiting:
        pending()
    shape = (columns_here, sequences)
    column_id = width_index * columns_here + lax.broadcasted_iota(jnp.int32, shape, 0)
    slab_id = lax.broadcasted_iota(jnp.int32, shape, 1)
    choose = jnp.zeros(shape, f32)
    for n in range(sequences):
        choose = jnp.where((slab_id == n) & (column_id == order_ref[n]), 1.0, choose)
    out_ref[...] = lax.dot_general(
        choose, scores[0], (((1,), (1,)), ((), ())), precision=highest
    )


def solve(halves, ids, order, prior_operands, bank_shape, grads, out_shape):
    size = grads.shape[2]
    rows = order.shape[0] + out_shape[1]
    copies = 2 + bank_shape[0] * (2 * bank_shape[0] + bank_shape[1])
    near = len(prior_operands) - 1 if halves else 0
    vmem = pl.BlockSpec(memory_space=pltpu.VMEM)
    scratch = [
        pltpu.VMEM((size, size), f32),
        pltpu.VMEM((rows, size), f32),
        pltpu.VMEM((BLOCK, BLOCK), f32),
        pltpu.VMEM((TERMS * BLOCK, size), jnp.bfloat16),
        pltpu.VMEM((TERMS * BLOCK, size), jnp.bfloat16),
    ]
    if halves:
        scratch.append(pltpu.VMEM((bank_shape[0], bank_shape[0], 8, 2 * BLOCK), f32))
    return pl.pallas_call(
        functools.partial(solve_kernel, halves),
        out_shape=jax.ShapeDtypeStruct(out_shape, f32),
        in_specs=[pl.BlockSpec(memory_space=pltpu.SMEM)] * 2
        + [pl.BlockSpec(memory_space=pltpu.HBM)] * (len(prior_operands) - near)
        + [vmem] * near
        + [vmem],
        out_specs=vmem,
        scratch_shapes=scratch
        + [pltpu.VMEM(bank_shape, f32), pltpu.SemaphoreType.DMA((copies,))],
        compiler_params=pltpu.CompilerParams(vmem_limit_bytes=52 * 2**20),
        cost_estimate=pl.CostEstimate(
            flops=4 * size**3, bytes_accessed=4 * size * size, transcendentals=size
        ),
    )(ids, order, *prior_operands, grads)


def local(
    layer_inputs,
    output_grads,
    proj_in,
    proj_out,
    prior_gram,
    query_bank,
    slab_sequence,
    seq_lengths,
    query_ids,
):
    width_count = lax.axis_size("width")
    token_count = lax.axis_size("tokens")
    token_index = lax.axis_index("tokens")
    slab_count = layer_inputs.shape[0] // SEQ_LEN
    sequence_count = slab_sequence.shape[0]
    bank_rows = query_bank.shape[0]
    halves = prior_gram.shape == (2 * BLOCK, 2 * BLOCK)

    if halves:
        half, first = pack(prior_gram, query_bank)
        own = lax.all_gather(first, "tokens", axis=0)
        pieces = [swap(half, "width", s) for s in range(1, width_count)]
        bank_shape = (token_count, query_bank.shape[1] // (2 * BLOCK), bank_rows, 2 * BLOCK)
    else:
        prior_block = lax.all_gather(prior_gram, "width", axis=1, tiled=True)
        prior_full = lax.all_gather(prior_block, "tokens", axis=0, tiled=True)
        bank_shape = (token_count, 1, bank_rows, query_bank.shape[1])
        bank_full = lax.all_gather(query_bank, "tokens", axis=0, tiled=True)
        prior_operands = (prior_full, bank_full.reshape(bank_shape))

    features = (((1,), (1,)), ((), ()))
    projected = jnp.concatenate(
        [
            lax.dot_general(proj_in, layer_inputs, features, preferred_element_type=f32),
            lax.dot_general(proj_out, output_grads, features, preferred_element_type=f32),
        ],
        axis=0,
    )
    total = projected + swap(projected, "width", 1)
    if halves:
        total, pieces = lax.optimization_barrier((total, pieces))
        pieces = jnp.concatenate(pieces, 0)
        across = swap(pieces, "tokens", 2)
        prior_operands = (
            own,
            pieces,
            swap(pieces, "tokens", 1),
            across,
            swap(across, "tokens", 1),
        )
    distance = 2
    while distance < width_count:
        total = total + swap(total, "width", distance)
        distance *= 2
    local_slabs = lax.dynamic_slice_in_dim(slab_sequence, token_index * slab_count, slab_count)
    seq_numbers = jnp.arange(sequence_count, dtype=jnp.int32)
    local_lengths = jnp.sum(
        jnp.where(local_slabs[:, None] == seq_numbers[None, :], seq_lengths[None, :], 0), axis=1
    )
    offset = jnp.arange(SEQ_LEN, dtype=jnp.int32)
    valid = (offset[None, :] < local_lengths[:, None]).reshape(1, -1)
    total_in = jnp.where(valid, total[:R_IN], 0.0).reshape(R_IN, slab_count, SEQ_LEN)
    total_out = total[R_IN:].reshape(-1, slab_count, SEQ_LEN)
    vectors = lax.dot_general(
        total_in, total_out, (((2,), (2,)), ((1,), (1,))), precision=highest
    ).reshape(slab_count, K)
    all_grads = lax.all_gather(vectors, "tokens", axis=0)
    out_shape = (sequence_count // width_count, query_ids.shape[0] // token_count)
    return solve(
        halves, query_ids, slab_sequence, prior_operands, bank_shape, all_grads, out_shape
    ).T


def solution(mesh):
    return jax.shard_map(
        local,
        mesh=mesh,
        in_specs=(
            P(("groups", "tokens"), "width"),
            P(("groups", "tokens"), "width"),
            P(None, "width"),
            P(None, "width"),
            P(("groups", "tokens"), "width"),
            P(("groups", "tokens"), None),
            P("groups"),
            P("groups"),
            P("groups"),
        ),
        out_specs=P(("groups", "tokens"), "width"),
        check_vma=False,
    )
```
